1024 devices in a mesh: seq: 128 (over z, y_hi, core), head: 8 (over x, y_lo).
Axes of the slice: x: 4, y: 4 (y_hi: 2, y_lo: 2; y = y_hi * 2 + y_lo), z: 32, core: 2. Of those that a mesh axis runs over, the one named last changes fastest.
Arguments:
- queries: bfloat16 [16384, 4096], P('seq', 'head'), may hold values from -192 to 192
- keys: bfloat16 [16384, 1024], P('seq', 'head'), may hold values from -5 to 5
- values: bfloat16 [16384, 1024], P('seq', 'head'), may hold values from -24 to 24
- segments: int32 [16384], replicated, may hold values from 0 to 5, never falling along the last dimension, each value on 1 to 5461 neighbouring positions
- out_weight: bfloat16 [4096, 8192], P(None, 'head'), may hold values from -0.09375 to 0.09375
Outputs:
- mixed: bfloat16 [16384, 8192], P('seq', 'head')
The draws below stay inside these ranges and needn't reach their ends.
All inputs are finite; a program needn't handle non-finite values.
Results may differ from the reference program's by a relative error of at most 0.007.
Values may be sent and summed in bfloat16 or wider, within the bound.
No kernel may reach another device: no remote copies, remote signals or barrier semaphores. Data moves between devices by JAX's collectives and lax.ppermute only.
A program may use at most 32 MiB of HBM per device.

```python
import math
import jax
import jax.numpy as jnp
import numpy as np
from jax import lax

D = 8192
HD = 128
GROUP = 4
TOK_DEV = 128
WIN_BLK = 31
KV_HEADS = 8
QH = 32
TOKENS = 16384


def drawn_rows(key):
    key_field = jax.random.normal(jax.random.fold_in(key, 11), (TOKENS, KV_HEADS, HD), jnp.float32)
    key_field = jnp.clip(key_field, -5.0, 5.0)
    return key_field


def draw_keys(key, part):
    key_field = drawn_rows(key)
    return key_field.reshape(TOKENS, KV_HEADS * HD).astype(jnp.bfloat16)


def draw_queries(key, part):
    base = jax.random.normal(jax.random.fold_in(key, 13), (TOKENS, KV_HEADS, GROUP, HD), jnp.float32)
    base = 2.0 * jnp.clip(base, -5.0, 5.0)
    return base.reshape(TOKENS, KV_HEADS * GROUP * HD).astype(jnp.bfloat16)


def level_of(stream_key, shape, shards, least, top_value):
    gain = 1.0
    for dim, shards_of in shards:
        heights = jax.random.uniform(jax.random.fold_in(jax.random.fold_in(stream_key, 6), dim), (shards_of,), jnp.float32, least / len(shards), top_value / len(shards))
        gain = gain * jnp.repeat(jnp.exp(heights), shape[dim] // shards_of).reshape((-1,) + (1,) * (len(shape) - 1 - dim))
    return gain


def split_up(amount, total, bound, slope):
    loads = [(1 << 20) // math.isqrt(grade ** slope) + 1 for grade in range(2, amount + 1)]
    surplus, given = total - bound - (amount - 1), [1] * (amount - 1)
    while surplus > 0:
        movable = [i for i in range(amount - 1) if given[i] < bound]
        mass, left = sum([loads[i] for i in movable]), surplus
        for i in movable:
            more = min(bound - given[i], max(1, left * loads[i] // mass), surplus)
            given[i] = given[i] + more
            surplus = surplus - more
    return np.array([bound] + given)


def ragged_sizes(own_key, count, total, most, lean):
    if count == 2:
        one = jax.random.randint(own_key, (), max(1, total - most), min(most, total - 1) + 1)
        return jnp.stack([one, total - one])
    tallies = jnp.asarray(split_up(count, total, most, lean), jnp.int32)
    pairs = (count - 1) // 2
    donor, receiver = tallies[1:1 + 2 * pairs:2], tallies[2:2 + 2 * pairs:2]
    margin = jnp.minimum(donor - 1, most - receiver)
    passed = jax.random.randint(jax.random.fold_in(own_key, 1), (pairs,), 0, 1 << 20) % (margin + 1)
    tallies = tallies.at[1:1 + 2 * pairs:2].set(donor - passed).at[2:2 + 2 * pairs:2].set(receiver + passed)
    return tallies[jax.random.permutation(jax.random.fold_in(own_key, 2), count)]


def normal_values(own_key, extent, scale, limit, pieces=(), kind=jnp.bfloat16):
    loudness = level_of(own_key, extent, pieces, -0.22, 0.18) if pieces else 1.0
    values = jax.random.normal(own_key, extent, jnp.float32) * scale * loudness
    return jnp.minimum(jnp.maximum(values, -limit), limit).astype(kind)


def setup_inputs(seed: int = 0) -> dict:
    splits = jax.random.split(jax.random.key(seed), 6)
    queries = draw_queries(jax.random.fold_in(splits[5], 71), 0)
    keys = draw_keys(jax.random.fold_in(splits[5], 71), 0)
    values = normal_values(splits[2], (TOKENS, KV_HEADS * HD), 4.0, 24.0, ((0, 128), (1, 8)))
    segments = jnp.searchsorted(jnp.cumsum(ragged_sizes(splits[3], 6, TOKENS, TOKENS // 3, 1)), jnp.arange(TOKENS), side="right").astype(jnp.int32)
    out_weight = normal_values(splits[4], (QH * HD, D), (QH * HD) ** -0.5, 0.09375, ((1, 8),))
    return dict(queries=queries, keys=keys, values=values, segments=segments, out_weight=out_weight)


masked_score = -1e+30

def reference(queries, keys, values, segments, out_weight):
    token_total = queries.shape[0]
    kv_heads = keys.shape[1] // HD
    group_size = queries.shape[1] // keys.shape[1]
    window_len = WIN_BLK * TOK_DEV
    length = window_len + TOK_DEV
    padding = jnp.zeros((window_len, keys.shape[1]), keys.dtype)
    keys_padded = jnp.concatenate([padding, keys], axis=0)
    values_padded = jnp.concatenate([padding, values], axis=0)
    seg_whole = segments.astype(jnp.int32)
    seg_padded = jnp.concatenate([jnp.full((window_len,), -1, jnp.int32), seg_whole])
    scaling = 1.0 / math.sqrt(HD)

    def one_block(block_index):
        first_row = (block_index * TOK_DEV).astype(jnp.int32)
        query_block = lax.dynamic_slice_in_dim(queries, first_row, TOK_DEV, 0)
        query_block = query_block.reshape(TOK_DEV, kv_heads, group_size, HD).astype(jnp.float32)
        key_block = lax.dynamic_slice_in_dim(keys_padded, first_row, length, 0)
        key_block = key_block.reshape(length, kv_heads, HD).astype(jnp.float32)
        value_block = lax.dynamic_slice_in_dim(values_padded, first_row, length, 0)
        value_block = value_block.reshape(length, kv_heads, HD).astype(jnp.float32)
        query_pos = first_row + jnp.arange(TOK_DEV, dtype=jnp.int32)
        key_pos = first_row - window_len + jnp.arange(length, dtype=jnp.int32)
        query_seg = lax.dynamic_slice_in_dim(seg_whole, first_row, TOK_DEV, 0)
        key_seg = lax.dynamic_slice_in_dim(seg_padded, first_row, length, 0)
        allowed = key_pos[None, :] <= query_pos[:, None]
        allowed = allowed & (query_pos[:, None] - key_pos[None, :] < window_len)
        allowed = allowed & (key_pos[None, :] >= 0)
        allowed = allowed & (key_seg[None, :] == query_seg[:, None])
        scores = jnp.einsum('tagd,sad->agts', query_block, key_block) * scaling
        scores = jnp.where(allowed[None, None], scores, masked_score)
        row_max = lax.optimization_barrier(jnp.max(scores, axis=-1, keepdims=True))
        weights = jnp.exp(scores - row_max)
        denominator = lax.optimization_barrier(jnp.sum(weights, axis=-1))
        rounded = lax.optimization_barrier(weights.astype(jnp.bfloat16)).astype(jnp.float32)
        numerator = jnp.einsum('agts,sad->tagd', rounded, value_block)
        result = numerator / jnp.transpose(denominator, (2, 0, 1))[..., None]
        return result.reshape(TOK_DEV, kv_heads * group_size * HD).astype(jnp.bfloat16)
    blocks = lax.map(one_block, jnp.arange(token_total // TOK_DEV, dtype=jnp.int32))
    attended = blocks.reshape(token_total, queries.shape[1])
    return jnp.dot(attended, out_weight, preferred_element_type=jnp.float32).astype(jnp.bfloat16)
```

```python
import functools

import jax
import jax.numpy as jnp
from jax import lax
from jax.experimental import pallas as pl
from jax.experimental.pallas import tpu as pltpu
from jax.sharding import Mesh, PartitionSpec as P

HD = 128
BLK = 128
GROUP = 4
LANES = 4
WINDOW = 31 * BLK
PLANE = LANES * BLK
ROWS = GROUP * BLK
PIECES = 16
HEADS = 8
SEGMENT_VALUES = 6
SCALE2 = float(HD**-0.5 * 1.4426950408889634)
MASKED = -1e30
VMEM = 24 * 1024 * 1024


def shift(block, distance):
    planes = lax.axis_size("z")
    return lax.ppermute(block, "z", [(i, i + distance) for i in range(planes - distance)])


def first_allowed(segments, plane):
    own = lax.dynamic_slice_in_dim(segments, plane * PLANE, PLANE, 0)
    position = plane * PLANE + jnp.arange(PLANE, dtype=jnp.int32)
    start = jnp.zeros((PLANE,), jnp.int32)
    for value in range(1, SEGMENT_VALUES):
        before = jnp.sum((segments < value).astype(jnp.int32))
        start = jnp.where(own == value, before, start)
    return jnp.maximum(start, position - (WINDOW - 1)).reshape(LANES, 1, BLK)


def attend(where_ref, q_ref, low_ref, blocks, distances, old_max):
    token_block = pl.program_id(0)
    own_key, plane_first = where_ref[0], where_ref[1]
    queries = jnp.concatenate([q_ref[0, :, g * HD : (g + 1) * HD] for g in range(GROUP)], axis=0)
    keys = jnp.concatenate([k for k in blocks], axis=0)
    scores = lax.dot_general(keys, queries, (((1,), (1,)), ((), ())), preferred_element_type=jnp.float32)
    low = jnp.concatenate([low_ref[0]] * GROUP, axis=1)
    sub = lax.broadcasted_iota(jnp.int32, (BLK, ROWS), 0)
    parts = []
    for n, distance in enumerate(distances):
        piece = scores[n * BLK : (n + 1) * BLK] * SCALE2
        first = own_key - distance * PLANE
        allowed = sub >= low - first
        if distance == 0:
            token = lax.broadcasted_iota(jnp.int32, (1, ROWS), 1) % BLK
            allowed = allowed & (sub <= plane_first + token_block * BLK + token - first)
        parts.append(jnp.where(allowed, piece, MASKED))
    top = functools.reduce(jnp.maximum, parts)
    top = jnp.max(top, axis=0, keepdims=True)
    if old_max is not None:
        top = jnp.maximum(top, old_max)
    weights = [jnp.exp2(piece - top) for piece in parts]
    total = jnp.sum(functools.reduce(jnp.add, weights), axis=0, keepdims=True)
    return top, total, jnp.concatenate([w.astype(jnp.bfloat16) for w in weights], axis=0)


def put_values(values_t, blocks):
    for n, block in enumerate(blocks):
        values_t[:, n * BLK : (n + 1) * BLK] = block.astype(jnp.float32).T.astype(jnp.bfloat16)


NEAR = (0, 1, 2, 3, 6)
FAR = (4, 7, 5, 8)


def near_kernel(where_ref, q_ref, low_ref, kv0, kv1, kv2, kv3, kv6, acc_ref, stat_ref, values_t):
    refs = (kv0, kv1, kv2, kv3, kv6)

    @pl.when(pl.program_id(0) == 0)
    def _():
        put_values(values_t, [r[:, HD:] for r in refs])

    top, total, weights = attend(where_ref, q_ref, low_ref, [r[:, :HD] for r in refs], NEAR, None)
    acc_ref[0] = jnp.dot(values_t[...], weights, preferred_element_type=jnp.float32)
    stat_ref[0, 0:1] = top
    stat_ref[0, 1:2] = total


def far_kernel(where_ref, q_ref, low_ref, one, two, acc_ref, stat_ref, out_ref, values_t):
    refs = (one, two)

    @pl.when(pl.program_id(0) == 0)
    def _():
        put_values(values_t, [r[i * BLK : (i + 1) * BLK, HD:] for r in refs for i in range(2)])

    old_max, old_total = stat_ref[0, 0:1], stat_ref[0, 1:2]
    keys = [r[:, :HD] for r in refs]
    top, total, weights = attend(where_ref, q_ref, low_ref, keys, FAR, old_max)
    factor = jnp.exp2(old_max - top)
    total = total + old_total * factor
    acc = acc_ref[0] * factor + jnp.dot(values_t[...], weights, preferred_element_type=jnp.float32)
    out_ref[0, :HD] = (acc / total).astype(jnp.bfloat16)
    spread = top + jnp.log2(total)
    high = spread.astype(jnp.bfloat16)
    rest = spread - high.astype(jnp.float32)
    middle = rest.astype(jnp.bfloat16)
    rest = rest - middle.astype(jnp.float32)
    row = lax.broadcasted_iota(jnp.int32, (PIECES, ROWS), 0)
    pieces = jnp.where(row == 0, high.astype(jnp.float32), jnp.where(row == 1, middle.astype(jnp.float32), jnp.where(row == 2, rest, 0.0)))
    out_ref[0, HD:] = pieces.astype(jnp.bfloat16)


def combine_kernel(parts_ref, out_ref):
    spread = []
    for p in range(LANES):
        pieces = parts_ref[p, HD:].astype(jnp.float32)
        spread.append(pieces[0:1] + pieces[1:2] + pieces[2:3])
    top = functools.reduce(jnp.maximum, spread)
    shares = [jnp.exp2(s - top) for s in spread]
    inverse = 1.0 / functools.reduce(jnp.add, shares)
    total = functools.reduce(
        jnp.add, [parts_ref[p, :HD].astype(jnp.float32) * (shares[p] * inverse) for p in range(LANES)]
    )
    for g in range(GROUP):
        head = total[:, g * BLK : (g + 1) * BLK].T.astype(jnp.bfloat16)
        for h in range(HEADS):
            out_ref[h, :, g * HD : (g + 1) * HD] = head


def project_kernel(rows_ref, weight_ref, out_ref, acc):
    step = pl.program_id(0)
    product = jnp.dot(rows_ref[0], weight_ref[...], preferred_element_type=jnp.float32)

    @pl.when(step == 0)
    def _():
        acc[...] = product

    @pl.when(step > 0)
    def _():
        acc[...] += product

    @pl.when(step == pl.num_programs(0) - 1)
    def _():
        out_ref[...] = acc[...].astype(jnp.bfloat16)


def whole(*shape):
    return pl.BlockSpec(shape, lambda i: (0,) * len(shape))


def stepped(*shape):
    return pl.BlockSpec((1, *shape), lambda i: (i,) + (0,) * len(shape))


def on_device(queries, keys, values, segments, out_weight):
    plane = lax.axis_index("z")
    lane = lax.axis_index("p")
    own = jnp.concatenate([keys, values], axis=1)
    from3, from6 = shift(own, 3), shift(own, 6)
    from1, from2 = shift(own, 1), shift(own, 2)
    pair = jnp.concatenate([from3, from6], axis=0)
    one, two = shift(pair, 1), shift(pair, 2)

    low = first_allowed(segments, plane)
    where = jnp.stack([plane * PLANE + lane * BLK, plane * PLANE]).astype(jnp.int32)
    plane_queries = lax.all_gather(queries, "p")

    smem = pl.BlockSpec(memory_space=pltpu.SMEM)
    params = pltpu.CompilerParams(vmem_limit_bytes=VMEM)
    acc, stat = pl.pallas_call(
        near_kernel,
        grid=(LANES,),
        out_shape=(
            jax.ShapeDtypeStruct((LANES, HD, ROWS), jnp.float32),
            jax.ShapeDtypeStruct((LANES, 8, ROWS), jnp.float32),
        ),
        in_specs=[smem, stepped(BLK, GROUP * HD), stepped(1, BLK)] + [whole(BLK, 2 * HD)] * 5,
        out_specs=(stepped(HD, ROWS), stepped(8, ROWS)),
        scratch_shapes=[pltpu.VMEM((HD, 5 * BLK), jnp.bfloat16)],
        compiler_params=params,
        cost_estimate=pl.CostEstimate(flops=4 * 2048 * 640 * 128, bytes_accessed=3 << 20, transcendentals=2048 * 640),
        name="near",
    )(where, plane_queries, low, own, from1, from2, from3, from6)
    partial = pl.pallas_call(
        far_kernel,
        grid=(LANES,),
        out_shape=jax.ShapeDtypeStruct((LANES, HD + PIECES, ROWS), jnp.bfloat16),
        in_specs=[smem, stepped(BLK, GROUP * HD), stepped(1, BLK)]
        + [whole(2 * BLK, 2 * HD)] * 2
        + [stepped(HD, ROWS), stepped(8, ROWS)],
        out_specs=stepped(HD + PIECES, ROWS),
        scratch_shapes=[pltpu.VMEM((HD, 4 * BLK), jnp.bfloat16)],
        compiler_params=params,
        cost_estimate=pl.CostEstimate(flops=4 * 2048 * 512 * 128, bytes_accessed=3 << 20, transcendentals=2048 * 512),
        name="far",
    )(where, plane_queries, low, one, two, acc, stat)
    parts = lax.all_to_all(partial, "p", 0, 0, tiled=True)
    copies = pl.pallas_call(
        combine_kernel,
        out_shape=jax.ShapeDtypeStruct((HEADS, BLK, GROUP * HD), jnp.bfloat16),
        compiler_params=params,
        cost_estimate=pl.CostEstimate(flops=4 * 128 * 512, bytes_accessed=2 << 20, transcendentals=2048),
        name="combine",
    )(parts)
    attended = lax.all_to_all(copies, "h", 0, 0, tiled=True)
    width = out_weight.shape[1]
    return pl.pallas_call(
        project_kernel,
        grid=(HEADS,),
        out_shape=jax.ShapeDtypeStruct((BLK, width), jnp.bfloat16),
        in_specs=[stepped(BLK, GROUP * HD), pl.BlockSpec((GROUP * HD, width), lambda i: (i, 0))],
        out_specs=whole(BLK, width),
        scratch_shapes=[pltpu.VMEM((BLK, width), jnp.float32)],
        compiler_params=params,
        cost_estimate=pl.CostEstimate(flops=2 * 128 * 4096 * 1024, bytes_accessed=9 << 20, transcendentals=0),
        name="project",
    )(attended, out_weight)


def solution(mesh):
    planes = mesh.shape["seq"] // LANES
    fine = Mesh(mesh.devices.reshape(planes, LANES, mesh.shape["head"]), ("z", "p", "h"))
    return jax.shard_map(
        on_device,
        mesh=fine,
        in_specs=(P(("z", "p"), "h"), P(("z", "p"), "h"), P(("z", "p"), "h"), P(), P(None, "h")),
        out_specs=P(("z", "p"), "h"),
        check_vma=False,
    )
```

```python
import functools

import jax
import jax.numpy as jnp
from jax import lax
from jax.experimental import pallas as pl
from jax.experimental.pallas import tpu as pltpu
from jax.sharding import Mesh, PartitionSpec as P

HD = 128
BLK = 128
GROUP = 4
PAIR = 2
LANES = 4
WINDOW = 31 * BLK
PLANE = LANES * BLK
ROWS = GROUP * BLK
PIECES = 16
HEADS = 8
SEGMENT_VALUES = 6
SCALE2 = float(HD**-0.5 * 1.4426950408889634)
MASKED = -1e30
VMEM = 24 * 1024 * 1024
PARAMS = pltpu.CompilerParams(vmem_limit_bytes=VMEM)
SMEM = pl.BlockSpec(memory_space=pltpu.SMEM)
VREF = pl.BlockSpec(memory_space=pltpu.VMEM)
STATE = (
    jax.ShapeDtypeStruct((LANES, HD, ROWS), jnp.float32),
    jax.ShapeDtypeStruct((LANES, 8, ROWS), jnp.float32),
)


def shift(block, distance):
    planes = lax.axis_size("z")
    return lax.ppermute(block, "z", [(i, i + distance) for i in range(planes - distance)])


def pack_kernel(key_ref, value_ref, out_ref, sems):
    key_copy = pltpu.make_async_copy(key_ref, out_ref.at[:, pl.ds(0, HD)], sems.at[0])
    value_copy = pltpu.make_async_copy(value_ref, out_ref.at[:, pl.ds(HD, HD)], sems.at[1])
    key_copy.start()
    value_copy.start()
    key_copy.wait()
    value_copy.wait()


def trio_kernel(own_ref, from3_ref, from6_ref, out_ref):
    for n, ref in enumerate((own_ref, from3_ref, from6_ref)):
        out_ref[n * BLK : (n + 1) * BLK] = ref[...]


def low_kernel(where_ref, segment_ref, out_ref):
    segments = segment_ref[...]
    before = [jnp.sum((segments < v).astype(jnp.int32)) for v in range(1, SEGMENT_VALUES)]
    token = lax.broadcasted_iota(jnp.int32, (1, BLK), 1)
    for p in range(LANES):
        own = segment_ref[pl.ds(where_ref[1] * LANES + p, 1), :]
        start = jnp.zeros((1, BLK), jnp.int32)
        for v in range(1, SEGMENT_VALUES):
            start = jnp.where(own == v, before[v - 1], start)
        position = where_ref[1] * PLANE + p * BLK + token
        out_ref[p : p + 1] = jnp.maximum(start, position - (WINDOW - 1))
    out_ref[LANES:] = jnp.zeros((8 - LANES, BLK), jnp.int32)


def attend_kernel(distances, first, last, where_ref, mine_ref, other_ref, low_ref, kv_ref, *refs):
    old, refs = ((), refs) if first else (refs[:2], refs[2:])
    own_key, plane_first, side = where_ref[0], where_ref[1] * PLANE, where_ref[2]
    keys = kv_ref[:, :HD]
    values_t = kv_ref[:, HD:].astype(jnp.float32).T.astype(jnp.bfloat16)
    sub = lax.broadcasted_iota(jnp.int32, (BLK, ROWS), 0)
    for index in range(LANES):
        query_ref, core = (mine_ref, other_ref)[index // PAIR], index % PAIR
        block = core + PAIR * (side if index < PAIR else 1 - side)
        rows = slice(core * BLK, (core + 1) * BLK)
        queries = jnp.concatenate([query_ref[rows, g * HD : (g + 1) * HD] for g in range(GROUP)], axis=0)
        scores = lax.dot_general(keys, queries, (((1,), (1,)), ((), ())), preferred_element_type=jnp.float32)
        low = jnp.concatenate([low_ref[pl.ds(block, 1), :]] * GROUP, axis=1)
        parts = []
        for n, distance in enumerate(distances):
            key_first = own_key - distance * PLANE
            allowed = sub >= low - key_first
            if distance == 0:
                token = lax.broadcasted_iota(jnp.int32, (1, ROWS), 1) % BLK
                allowed = allowed & (sub <= plane_first + block * BLK + token - key_first)
            parts.append(jnp.where(allowed, scores[n * BLK : (n + 1) * BLK] * SCALE2, MASKED))
        top = jnp.max(functools.reduce(jnp.maximum, parts), axis=0, keepdims=True)
        if not first:
            old_top = old[1][index, 0:1]
            top = jnp.maximum(top, old_top)
        weights = [jnp.exp2(piece - top) for piece in parts]
        total = jnp.sum(functools.reduce(jnp.add, weights), axis=0, keepdims=True)
        weights = jnp.concatenate([w.astype(jnp.bfloat16) for w in weights], axis=0)
        acc = jnp.dot(values_t, weights, preferred_element_type=jnp.float32)
        if not first:
            factor = jnp.exp2(old_top - top)
            total = total + old[1][index, 1:2] * factor
            acc = acc + old[0][index] * factor
        if not last:
            refs[0][index] = acc
            refs[1][index, 0:1] = top
            refs[1][index, 1:2] = total
            continue
        refs[0][block, :HD] = (acc / total).astype(jnp.bfloat16)
        spread = top + jnp.log2(total)
        high = spread.astype(jnp.bfloat16)
        rest = spread - high.astype(jnp.float32)
        middle = rest.astype(jnp.bfloat16)
        rest = rest - middle.astype(jnp.float32)
        row = lax.broadcasted_iota(jnp.int32, (PIECES, ROWS), 0)
        pieces = jnp.where(row == 0, high.astype(jnp.float32), jnp.where(row == 1, middle.astype(jnp.float32), jnp.where(row == 2, rest, 0.0)))
        refs[0][block, HD:] = pieces.astype(jnp.bfloat16)


def attend(name, distances, first, last, *args):
    out = jax.ShapeDtypeStruct((LANES, HD + PIECES, ROWS), jnp.bfloat16) if last else STATE
    pairs = LANES * ROWS * len(distances) * BLK
    return pl.pallas_call(
        functools.partial(attend_kernel, distances, first, last),
        out_shape=out,
        in_specs=[SMEM] + [VREF] * (len(args) - 1),
        out_specs=VREF if last else (VREF, VREF),
        compiler_params=PARAMS,
        cost_estimate=pl.CostEstimate(flops=4 * pairs * HD, bytes_accessed=3 << 20, transcendentals=pairs),
        name=name,
    )(*args)


def combine_kernel(parts_ref, out_ref):
    spread = []
    for p in range(LANES):
        pieces = parts_ref[p, HD:].astype(jnp.float32)
        spread.append(pieces[0:1] + pieces[1:2] + pieces[2:3])
    top = functools.reduce(jnp.maximum, spread)
    shares = [jnp.exp2(s - top) for s in spread]
    inverse = 1.0 / functools.reduce(jnp.add, shares)
    total = functools.reduce(
        jnp.add, [parts_ref[p, :HD].astype(jnp.float32) * (shares[p] * inverse) for p in range(LANES)]
    )
    for g in range(GROUP):
        head = total[:, g * BLK : (g + 1) * BLK].T.astype(jnp.bfloat16)
        for h in range(HEADS):
            out_ref[h, :, g * HD : (g + 1) * HD] = head


def project_kernel(rows_ref, weight_ref, out_ref):
    depth = rows_ref.shape[2]
    acc = functools.reduce(
        jnp.add,
        [
            jnp.dot(rows_ref[h], weight_ref[h * depth : (h + 1) * depth, :], preferred_element_type=jnp.float32)
            for h in range(HEADS)
        ],
    )
    out_ref[...] = acc.astype(jnp.bfloat16)


def small(kernel, name, shape, dtype, *args, smem=0, params=PARAMS):
    return pl.pallas_call(
        kernel,
        out_shape=jax.ShapeDtypeStruct(shape, dtype),
        in_specs=[SMEM] * smem + [VREF] * (len(args) - smem),
        out_specs=VREF,
        compiler_params=params,
        cost_estimate=pl.CostEstimate(flops=1 << 20, bytes_accessed=1 << 19, transcendentals=0),
        name=name,
    )(*args)


def pack(keys, values):
    return pl.pallas_call(
        pack_kernel,
        out_shape=jax.ShapeDtypeStruct((BLK, 2 * HD), keys.dtype),
        in_specs=[pl.BlockSpec(memory_space=pltpu.HBM)] * 2,
        out_specs=VREF,
        scratch_shapes=[pltpu.SemaphoreType.DMA((2,))],
        compiler_params=PARAMS,
        cost_estimate=pl.CostEstimate(flops=0, bytes_accessed=1 << 17, transcendentals=0),
        name="pack",
    )(keys, values)


def on_device(queries, keys, values, segments, out_weight):
    plane, side, core = lax.axis_index("z"), lax.axis_index("y"), lax.axis_index("c")
    where = jnp.stack([plane * PLANE + (side * PAIR + core) * BLK, plane, side]).astype(jnp.int32)
    own = pack(keys, values)
    from6 = shift(own, 6)
    from3 = shift(own, 3)
    queries, _ = lax.optimization_barrier((queries, own))
    mine = lax.all_gather(queries, "c", tiled=True)
    ready, _, _ = lax.optimization_barrier((mine, from3, from6))
    other = lax.ppermute(ready, "y", [(0, 1), (1, 0)])
    low = small(low_kernel, "low", (8, BLK), jnp.int32, where, segments.reshape(-1, BLK), smem=1)
    trio = small(trio_kernel, "trio", (3 * BLK, 2 * HD), keys.dtype, own, from3, from6)
    one, two = shift(trio, 1), shift(trio, 2)
    common = (where, mine, other, low)
    state = attend("near", (0, 3, 6), True, False, *common, trio)
    state = attend("middle", (1, 4, 7), False, False, *common, one, *state)
    partial = attend("far", (2, 5, 8), False, True, *common, two, *state)
    parts = lax.all_to_all(partial, ("y", "c"), 0, 0, tiled=True)
    copies = small(combine_kernel, "combine", (HEADS, BLK, GROUP * HD), jnp.bfloat16, parts)
    attended = lax.all_to_all(copies, "h", 0, 0, tiled=True)
    return small(project_kernel, "project", (BLK, out_weight.shape[1]), jnp.bfloat16, attended, out_weight)


def solution(mesh):
    planes = mesh.shape["seq"] // LANES
    heads = mesh.shape["head"]
    fine = Mesh(mesh.devices.reshape(planes, LANES // PAIR, PAIR, heads), ("z", "y", "c", "h"))
    tokens = ("z", "y", "c")
    return jax.shard_map(
        on_device,
        mesh=fine,
        in_specs=(P(tokens, "h"), P(tokens, "h"), P(tokens, "h"), P(), P(None, "h")),
        out_specs=P(tokens, "h"),
        check_vma=False,
    )
```

```python
import functools

import jax
import jax.numpy as jnp
from jax import lax
from jax.experimental import pallas as pl
from jax.experimental.pallas import tpu as pltpu
from jax.sharding import Mesh, PartitionSpec as P

HD = 128
BLK = 128
GROUP = 4
PAIR = 2
LANES = 4
WINDOW = 31 * BLK
PLANE = LANES * BLK
ROWS = GROUP * BLK
PIECES = 16
HEADS = 8
SEGMENT_VALUES = 6
SCALE2 = float(HD**-0.5 * 1.4426950408889634)
MASKED = -1e30
VMEM = 24 * 1024 * 1024
PARAMS = pltpu.CompilerParams(vmem_limit_bytes=VMEM)
SMEM = pl.BlockSpec(memory_space=pltpu.SMEM)
VREF = pl.BlockSpec(memory_space=pltpu.VMEM)
STATE = (
    jax.ShapeDtypeStruct((LANES, HD, ROWS), jnp.float32),
    jax.ShapeDtypeStruct((LANES, 8, ROWS), jnp.float32),
)


def shift_by_core(block, distances):
    planes, cores = lax.axis_size("z"), lax.axis_size("c")
    route = [
        (z * cores + c, (z + distances[c]) * cores + c) for c in range(cores) for z in range(planes - distances[c])
    ]
    return lax.ppermute(block, ("z", "c"), route)


def pack_kernel(key_ref, value_ref, out_ref, sems):
    key_copy = pltpu.make_async_copy(key_ref, out_ref.at[:, pl.ds(0, HD)], sems.at[0])
    value_copy = pltpu.make_async_copy(value_ref, out_ref.at[:, pl.ds(HD, HD)], sems.at[1])
    key_copy.start()
    value_copy.start()
    key_copy.wait()
    value_copy.wait()


def join_kernel(own_ref, come_ref, out_ref):
    rows = own_ref.shape[0]
    out_ref[:rows] = own_ref[...]
    out_ref[rows:] = come_ref[...]


def low_kernel(where_ref, segment_ref, out_ref):
    segments = segment_ref[...]
    before = [jnp.sum((segments < v).astype(jnp.int32)) for v in range(1, SEGMENT_VALUES)]
    token = lax.broadcasted_iota(jnp.int32, (1, BLK), 1)
    for p in range(LANES):
        own = segment_ref[pl.ds(where_ref[0] * LANES + p, 1), :]
        start = jnp.zeros((1, BLK), jnp.int32)
        for v in range(1, SEGMENT_VALUES):
            start = jnp.where(own == v, before[v - 1], start)
        position = where_ref[0] * PLANE + p * BLK + token
        out_ref[p : p + 1] = jnp.maximum(start, position - (WINDOW - 1))
    out_ref[LANES:] = jnp.zeros((8 - LANES, BLK), jnp.int32)


def attend_kernel(near, where_ref, mine_ref, other_ref, low_ref, kv_ref, *refs):
    old, refs = ((), refs) if near else (refs[:2], refs[2:])
    plane, side, own_core = where_ref[0], where_ref[1], where_ref[2]
    plane_first = plane * PLANE
    side_first = plane_first + side * (PAIR * BLK)
    if near:
        firsts = [side_first + own_core * BLK - d * PLANE for d in (0, 3, 6)]
        held = jnp.concatenate(
            [kv_ref[pl.ds(pl.multiple_of((n * PAIR + own_core) * BLK, BLK), BLK), :] for n in range(3)], axis=0
        )
    else:
        firsts = [side_first + lane * BLK - (d + own_core) * PLANE for d in (1, 4, 7) for lane in range(PAIR)]
        held = kv_ref[...]
    keys = held[:, :HD]
    values_t = held[:, HD:].astype(jnp.float32).T.astype(jnp.bfloat16)
    sub = lax.broadcasted_iota(jnp.int32, (BLK, ROWS), 0)
    for index in range(LANES):
        query_ref, core = (mine_ref, other_ref)[index // PAIR], index % PAIR
        block = core + PAIR * (side if index < PAIR else 1 - side)
        rows = slice(core * BLK, (core + 1) * BLK)
        queries = jnp.concatenate([query_ref[rows, g * HD : (g + 1) * HD] for g in range(GROUP)], axis=0)
        scores = lax.dot_general(keys, queries, (((1,), (1,)), ((), ())), preferred_element_type=jnp.float32)
        low = jnp.concatenate([low_ref[pl.ds(block, 1), :]] * GROUP, axis=1)
        parts = []
        for n, key_first in enumerate(firsts):
            allowed = sub >= low - key_first
            if near and n == 0:
                token = lax.broadcasted_iota(jnp.int32, (1, ROWS), 1) % BLK
                allowed = allowed & (sub <= plane_first + block * BLK + token - key_first)
            parts.append(jnp.where(allowed, scores[n * BLK : (n + 1) * BLK] * SCALE2, MASKED))
        top = jnp.max(functools.reduce(jnp.maximum, parts), axis=0, keepdims=True)
        if not near:
            old_top = old[1][index, 0:1]
            top = jnp.maximum(top, old_top)
        weights = [jnp.exp2(piece - top) for piece in parts]
        total = jnp.sum(functools.reduce(jnp.add, weights), axis=0, keepdims=True)
        weights = jnp.concatenate([w.astype(jnp.bfloat16) for w in weights], axis=0)
        acc = jnp.dot(values_t, weights, preferred_element_type=jnp.float32)
        if not near:
            factor = jnp.exp2(old_top - top)
            total = total + old[1][index, 1:2] * factor
            acc = acc + old[0][index] * factor
        if near:
            refs[0][index] = acc
            refs[1][index, 0:1] = top
            refs[1][index, 1:2] = total
            continue
        refs[0][block, :HD] = (acc / total).astype(jnp.bfloat16)
        spread = top + jnp.log2(total)
        high = spread.astype(jnp.bfloat16)
        rest = spread - high.astype(jnp.float32)
        middle = rest.astype(jnp.bfloat16)
        rest = rest - middle.astype(jnp.float32)
        row = lax.broadcasted_iota(jnp.int32, (PIECES, ROWS), 0)
        pieces = jnp.where(row == 0, high.astype(jnp.float32), jnp.where(row == 1, middle.astype(jnp.float32), jnp.where(row == 2, rest, 0.0)))
        refs[0][block, HD:] = pieces.astype(jnp.bfloat16)


def attend(name, near, *args):
    out = STATE if near else jax.ShapeDtypeStruct((LANES, HD + PIECES, ROWS), jnp.bfloat16)
    pairs = LANES * ROWS * (3 if near else 6) * BLK
    return pl.pallas_call(
        functools.partial(attend_kernel, near),
        out_shape=out,
        in_specs=[SMEM] + [VREF] * (len(args) - 1),
        out_specs=(VREF, VREF) if near else VREF,
        compiler_params=PARAMS,
        cost_estimate=pl.CostEstimate(flops=4 * pairs * HD, bytes_accessed=3 << 20, transcendentals=pairs),
        name=name,
    )(*args)


def combine_kernel(parts_ref, out_ref):
    spread = []
    for p in range(LANES):
        pieces = parts_ref[p, HD:].astype(jnp.float32)
        spread.append(pieces[0:1] + pieces[1:2] + pieces[2:3])
    top = functools.reduce(jnp.maximum, spread)
    shares = [jnp.exp2(s - top) for s in spread]
    inverse = 1.0 / functools.reduce(jnp.add, shares)
    total = functools.reduce(
        jnp.add, [parts_ref[p, :HD].astype(jnp.float32) * (shares[p] * inverse) for p in range(LANES)]
    )
    for g in range(GROUP):
        head = total[:, g * BLK : (g + 1) * BLK].T.astype(jnp.bfloat16)
        for h in range(HEADS):
            out_ref[h, :, g * HD : (g + 1) * HD] = head


def project_kernel(rows_ref, weight_ref, out_ref):
    depth = rows_ref.shape[2]
    acc = functools.reduce(
        jnp.add,
        [
            jnp.dot(rows_ref[h], weight_ref[h * depth : (h + 1) * depth, :], preferred_element_type=jnp.float32)
            for h in range(HEADS)
        ],
    )
    out_ref[...] = acc.astype(jnp.bfloat16)


def small(kernel, name, shape, dtype, *args, smem=0, params=PARAMS):
    return pl.pallas_call(
        kernel,
        out_shape=jax.ShapeDtypeStruct(shape, dtype),
        in_specs=[SMEM] * smem + [VREF] * (len(args) - smem),
        out_specs=VREF,
        compiler_params=params,
        cost_estimate=pl.CostEstimate(flops=1 << 20, bytes_accessed=1 << 19, transcendentals=0),
        name=name,
    )(*args)


def pack(keys, values):
    return pl.pallas_call(
        pack_kernel,
        out_shape=jax.ShapeDtypeStruct((BLK, 2 * HD), keys.dtype),
        in_specs=[pl.BlockSpec(memory_space=pltpu.HBM)] * 2,
        out_specs=VREF,
        scratch_shapes=[pltpu.SemaphoreType.DMA((2,))],
        compiler_params=PARAMS,
        cost_estimate=pl.CostEstimate(flops=0, bytes_accessed=1 << 17, transcendentals=0),
        name="pack",
    )(keys, values)


def on_device(queries, keys, values, segments, out_weight):
    plane, side, core = lax.axis_index("z"), lax.axis_index("y"), lax.axis_index("c")
    where = jnp.stack([plane, side, core]).astype(jnp.int32)
    own = lax.all_gather(pack(keys, values), "c", tiled=True)
    low = small(low_kernel, "low", (8, BLK), jnp.int32, where, segments.reshape(-1, BLK), smem=1)
    come, low = lax.optimization_barrier((shift_by_core(own, (3, 6)), low))
    come = lax.all_gather(come, "c", tiled=True)
    queries, _ = lax.optimization_barrier((queries, own))
    mine = lax.all_gather(queries, "c", tiled=True)
    held = small(join_kernel, "join", (6 * BLK, 2 * HD), keys.dtype, own, come)
    far = shift_by_core(held, (1, 2))
    other = lax.ppermute(mine, "y", [(0, 1), (1, 0)])
    state = attend("near", True, where, mine, other, low, held)
    partial = attend("far", False, where, mine, other, low, far, *state)
    parts = lax.all_to_all(partial, ("y", "c"), 0, 0, tiled=True)
    copies = small(combine_kernel, "combine", (HEADS, BLK, GROUP * HD), jnp.bfloat16, parts)
    attended = lax.all_to_all(copies, "h", 0, 0, tiled=True)
    return small(project_kernel, "project", (BLK, out_weight.shape[1]), jnp.bfloat16, attended, out_weight)


def solution(mesh):
    planes = mesh.shape["seq"] // LANES
    heads = mesh.shape["head"]
    fine = Mesh(mesh.devices.reshape(planes, LANES // PAIR, PAIR, heads), ("z", "y", "c", "h"))
    tokens = ("z", "y", "c")
    return jax.shard_map(
        on_device,
        mesh=fine,
        in_specs=(P(tokens, "h"), P(tokens, "h"), P(tokens, "h"), P(), P(None, "h")),
        out_specs=P(tokens, "h"),
        check_vma=False,
    )
```

```python
import functools

import jax
import jax.numpy as jnp
from jax import lax
from jax.experimental import pallas as pl
from jax.experimental.pallas import tpu as pltpu
from jax.sharding import Mesh, PartitionSpec as P

HD = 128
BLK = 128
GROUP = 4
LANES = 4
WINDOW = 31 * BLK
PLANE = LANES * BLK
ROWS = GROUP * BLK
PIECES = 16
HEADS = 8
SEGMENT_VALUES = 6
SCALE2 = float(HD**-0.5 * 1.4426950408889634)
MASKED = -1e30
UNROLL = LANES
VMEM = 24 * 1024 * 1024
PARAMS = pltpu.CompilerParams(vmem_limit_bytes=VMEM)
SMEM = pl.BlockSpec(memory_space=pltpu.SMEM)
VREF = pl.BlockSpec(memory_space=pltpu.VMEM)
STATE = (
    jax.ShapeDtypeStruct((LANES, HD, ROWS), jnp.float32),
    jax.ShapeDtypeStruct((LANES, 8, ROWS), jnp.float32),
)


def shift(block, distance):
    planes = lax.axis_size("z")
    return lax.ppermute(block, "z", [(i, i + distance) for i in range(planes - distance)])


def pack_kernel(key_ref, value_ref, out_ref, sems):
    key_copy = pltpu.make_async_copy(key_ref, out_ref.at[:, pl.ds(0, HD)], sems.at[0])
    value_copy = pltpu.make_async_copy(value_ref, out_ref.at[:, pl.ds(HD, HD)], sems.at[1])
    key_copy.start()
    value_copy.start()
    key_copy.wait()
    value_copy.wait()


def trio_kernel(own_ref, from3_ref, from6_ref, out_ref):
    for n, ref in enumerate((own_ref, from3_ref, from6_ref)):
        out_ref[n * BLK : (n + 1) * BLK] = ref[...]


def low_kernel(where_ref, segment_ref, out_ref):
    segments = segment_ref[...]
    before = [jnp.sum((segments < v).astype(jnp.int32)) for v in range(1, SEGMENT_VALUES)]
    token = lax.broadcasted_iota(jnp.int32, (1, BLK), 1)
    for p in range(LANES):
        own = segment_ref[pl.ds(where_ref[0] * LANES + p, 1), :]
        start = jnp.zeros((1, BLK), jnp.int32)
        for v in range(1, SEGMENT_VALUES):
            start = jnp.where(own == v, before[v - 1], start)
        position = where_ref[0] * PLANE + p * BLK + token
        out_ref[p : p + 1] = jnp.maximum(start, position - (WINDOW - 1))
    out_ref[LANES:] = jnp.zeros((8 - LANES, BLK), jnp.int32)


def attend_kernel(distances, first, last, where_ref, query_ref, low_ref, kv_ref, *refs):
    old, refs = ((), refs) if first else (refs[:2], refs[2:])
    plane_first = where_ref[0] * PLANE
    own_first = plane_first + where_ref[1] * BLK
    keys = kv_ref[:, :HD]
    values_t = kv_ref[:, HD:].astype(jnp.float32).T.astype(jnp.bfloat16)
    sub = lax.broadcasted_iota(jnp.int32, (BLK, ROWS), 0)
    token = lax.broadcasted_iota(jnp.int32, (1, ROWS), 1) % BLK

    def one_block(block, carry):
        rows = pl.ds(pl.multiple_of(block * BLK, BLK), BLK)
        queries = jnp.concatenate([query_ref[rows, g * HD : (g + 1) * HD] for g in range(GROUP)], axis=0)
        scores = lax.dot_general(keys, queries, (((1,), (1,)), ((), ())), preferred_element_type=jnp.float32)
        low = jnp.concatenate([low_ref[pl.ds(block, 1), :]] * GROUP, axis=1)
        parts = []
        for n, distance in enumerate(distances):
            key_first = own_first - distance * PLANE
            allowed = sub >= low - key_first
            if distance == 0:
                allowed = allowed & (sub <= plane_first + block * BLK + token - key_first)
            parts.append(jnp.where(allowed, scores[n * BLK : (n + 1) * BLK] * SCALE2, MASKED))
        top = jnp.max(functools.reduce(jnp.maximum, parts), axis=0, keepdims=True)
        if not first:
            old_top = old[1][block, 0:1]
            top = jnp.maximum(top, old_top)
        weights = [jnp.exp2(piece - top) for piece in parts]
        total = jnp.sum(functools.reduce(jnp.add, weights), axis=0, keepdims=True)
        weights = jnp.concatenate([w.astype(jnp.bfloat16) for w in weights], axis=0)
        acc = jnp.dot(values_t, weights, preferred_element_type=jnp.float32)
        if not first:
            factor = jnp.exp2(old_top - top)
            total = total + old[1][block, 1:2] * factor
            acc = acc + old[0][block] * factor
        if not last:
            refs[0][block] = acc
            refs[1][block, 0:1] = top
            refs[1][block, 1:2] = total
            return carry
        refs[0][block, :HD] = (acc * (1.0 / total)).astype(jnp.bfloat16)
        spread = top + jnp.log2(total)
        high = spread.astype(jnp.bfloat16).astype(jnp.float32)
        rest = spread - high
        middle = rest.astype(jnp.bfloat16).astype(jnp.float32)
        row = lax.broadcasted_iota(jnp.int32, (PIECES, ROWS), 0)
        pieces = jnp.where(row == 0, high, jnp.where(row == 1, middle, jnp.where(row == 2, rest - middle, 0.0)))
        refs[0][block, HD:] = pieces.astype(jnp.bfloat16)
        return carry

    lax.fori_loop(0, LANES, one_block, 0, unroll=UNROLL)


def attend(name, distances, first, last, *args):
    out = jax.ShapeDtypeStruct((LANES, HD + PIECES, ROWS), jnp.bfloat16) if last else STATE
    pairs = LANES * ROWS * len(distances) * BLK
    return pl.pallas_call(
        functools.partial(attend_kernel, distances, first, last),
        out_shape=out,
        in_specs=[SMEM] + [VREF] * (len(args) - 1),
        out_specs=VREF if last else (VREF, VREF),
        compiler_params=PARAMS,
        cost_estimate=pl.CostEstimate(flops=4 * pairs * HD, bytes_accessed=3 << 20, transcendentals=pairs),
        name=name,
    )(*args)


def combine_kernel(parts_ref, out_ref):
    spread = []
    for p in range(LANES):
        pieces = parts_ref[p, HD:].astype(jnp.float32)
        spread.append(pieces[0:1] + pieces[1:2] + pieces[2:3])
    top = functools.reduce(jnp.maximum, spread)
    shares = [jnp.exp2(s - top) for s in spread]
    inverse = 1.0 / functools.reduce(jnp.add, shares)
    total = functools.reduce(
        jnp.add, [parts_ref[p, :HD].astype(jnp.float32) * (shares[p] * inverse) for p in range(LANES)]
    )
    for g in range(GROUP):
        head = total[:, g * BLK : (g + 1) * BLK].T.astype(jnp.bfloat16)
        for h in range(HEADS):
            out_ref[h, :, g * HD : (g + 1) * HD] = head


def project_kernel(rows_ref, weight_ref, out_ref):
    depth = rows_ref.shape[2]
    acc = functools.reduce(
        jnp.add,
        [
            jnp.dot(rows_ref[h], weight_ref[h * depth : (h + 1) * depth, :], preferred_element_type=jnp.float32)
            for h in range(HEADS)
        ],
    )
    out_ref[...] = acc.astype(jnp.bfloat16)


def small(kernel, name, shape, dtype, *args, smem=0, params=PARAMS):
    return pl.pallas_call(
        kernel,
        out_shape=jax.ShapeDtypeStruct(shape, dtype),
        in_specs=[SMEM] * smem + [VREF] * (len(args) - smem),
        out_specs=VREF,
        compiler_params=params,
        cost_estimate=pl.CostEstimate(flops=1 << 20, bytes_accessed=1 << 19, transcendentals=0),
        name=name,
    )(*args)


def pack(keys, values):
    return pl.pallas_call(
        pack_kernel,
        out_shape=jax.ShapeDtypeStruct((BLK, 2 * HD), keys.dtype),
        in_specs=[pl.BlockSpec(memory_space=pltpu.HBM)] * 2,
        out_specs=VREF,
        scratch_shapes=[pltpu.SemaphoreType.DMA((2,))],
        compiler_params=PARAMS,
        cost_estimate=pl.CostEstimate(flops=0, bytes_accessed=1 << 17, transcendentals=0),
        name="pack",
    )(keys, values)


def on_device(queries, keys, values, segments, out_weight):
    plane, lane = lax.axis_index("z"), lax.axis_index("p")
    where = jnp.stack([plane, lane]).astype(jnp.int32)
    low = small(low_kernel, "low", (8, BLK), jnp.int32, where, segments.reshape(-1, BLK), smem=1)
    own = pack(keys, values)
    queries, _ = lax.optimization_barrier((queries, own))
    plane_queries = lax.all_gather(queries, "p", tiled=True)
    from3, low = lax.optimization_barrier((shift(own, 3), low))
    from6, plane_queries = lax.optimization_barrier((shift(from3, 3), plane_queries))
    trio = small(trio_kernel, "trio", (3 * BLK, 2 * HD), keys.dtype, own, from3, from6)
    one, two = shift(trio, 1), shift(trio, 2)
    common = (where, plane_queries, low)
    state = attend("near", (0, 3, 6), True, False, *common, trio)
    state = attend("middle", (1, 4, 7), False, False, *common, one, *state)
    partial = attend("far", (2, 5, 8), False, True, *common, two, *state)
    parts = lax.all_to_all(partial, "p", 0, 0, tiled=True)
    copies = small(combine_kernel, "combine", (HEADS, BLK, GROUP * HD), jnp.bfloat16, parts)
    attended = lax.all_to_all(copies, "h", 0, 0, tiled=True)
    return small(project_kernel, "project", (BLK, out_weight.shape[1]), jnp.bfloat16, attended, out_weight)


def solution(mesh):
    planes = mesh.shape["seq"] // LANES
    fine = Mesh(mesh.devices.reshape(planes, LANES, mesh.shape["head"]), ("z", "p", "h"))
    tokens = ("z", "p")
    return jax.shard_map(
        on_device,
        mesh=fine,
        in_specs=(P(tokens, "h"), P(tokens, "h"), P(tokens, "h"), P(), P(None, "h")),
        out_specs=P(tokens, "h"),
        check_vma=False,
    )
```

```python
import functools

import jax
import jax.numpy as jnp
from jax import lax
from jax.experimental import pallas as pl
from jax.experimental.pallas import tpu as pltpu
from jax.sharding import Mesh, PartitionSpec as P

HD = 128
BLK = 128
GROUP = 4
PAIR = 2
LANES = 4
WINDOW = 31 * BLK
PLANE = LANES * BLK
ROWS = GROUP * BLK
PIECES = 16
HEADS = 8
SEGMENT_VALUES = 6
SCALE2 = float(HD**-0.5 * 1.4426950408889634)
MASKED = -1e30
UNROLL = LANES
VMEM = 24 * 1024 * 1024
PARAMS = pltpu.CompilerParams(vmem_limit_bytes=VMEM)
SMEM = pl.BlockSpec(memory_space=pltpu.SMEM)
VREF = pl.BlockSpec(memory_space=pltpu.VMEM)
STATE = (
    jax.ShapeDtypeStruct((LANES, HD, ROWS), jnp.float32),
    jax.ShapeDtypeStruct((LANES, 8, ROWS), jnp.float32),
)


def shift_by_core(block, distances):
    planes, cores = lax.axis_size("z"), lax.axis_size("c")
    route = [
        (z * cores + c, (z + distances[c]) * cores + c) for c in range(cores) for z in range(planes - distances[c])
    ]
    return lax.ppermute(block, ("z", "c"), route)


def pack_kernel(key_ref, value_ref, out_ref):
    out_ref[:, :HD] = key_ref[...]
    out_ref[:, HD:] = value_ref[...]


def low_kernel(where_ref, segment_ref, out_ref):
    segments = segment_ref[...]
    before = [jnp.sum((segments < v).astype(jnp.int32)) for v in range(1, SEGMENT_VALUES)]
    token = lax.broadcasted_iota(jnp.int32, (1, BLK), 1)
    for p in range(LANES):
        own = segment_ref[pl.ds(where_ref[0] * LANES + p, 1), :]
        start = jnp.zeros((1, BLK), jnp.int32)
        for v in range(1, SEGMENT_VALUES):
            start = jnp.where(own == v, before[v - 1], start)
        position = where_ref[0] * PLANE + p * BLK + token
        out_ref[p : p + 1] = jnp.maximum(start, position - (WINDOW - 1))
    out_ref[LANES:] = jnp.zeros((8 - LANES, BLK), jnp.int32)


def attend_kernel(near, where_ref, query_ref, low_ref, *refs):
    first, last = near, not near
    plane, lane = where_ref[0], where_ref[1]
    core = lane % PAIR
    plane_first = plane * PLANE
    side_first = plane_first + (lane - core) * BLK
    if near:
        own_ref, *pairs = refs[:3]
        old, refs = (), refs[3:]
        own_row = pl.multiple_of(core * BLK, BLK)
        blocks, firsts = [own_ref[pl.ds(own_row, BLK), :]], [side_first + own_row]
        distances = (1 + core, 3 + 3 * core)
    else:
        pairs, old, refs = refs[:2], refs[2:4], refs[4:]
        blocks, firsts = [], []
        distances = (4 + 3 * core, 5 + 3 * core)
    for ref, distance in zip(pairs, distances):
        blocks.append(ref[...])
        firsts += [side_first + n * BLK - distance * PLANE for n in range(PAIR)]
    held = jnp.concatenate(blocks, axis=0)
    keys = held[:, :HD]
    values_t = held[:, HD:].astype(jnp.float32).T.astype(jnp.bfloat16)
    sub = lax.broadcasted_iota(jnp.int32, (BLK, ROWS), 0)
    token = lax.broadcasted_iota(jnp.int32, (1, ROWS), 1) % BLK

    def one_block(block, carry):
        rows = pl.ds(pl.multiple_of(block * BLK, BLK), BLK)
        queries = jnp.concatenate([query_ref[rows, g * HD : (g + 1) * HD] for g in range(GROUP)], axis=0)
        scores = lax.dot_general(keys, queries, (((1,), (1,)), ((), ())), preferred_element_type=jnp.float32)
        low = jnp.concatenate([low_ref[pl.ds(block, 1), :]] * GROUP, axis=1)
        parts = []
        for n, key_first in enumerate(firsts):
            allowed = sub >= low - key_first
            if near and n == 0:
                allowed = allowed & (sub <= plane_first + block * BLK + token - key_first)
            parts.append(jnp.where(allowed, scores[n * BLK : (n + 1) * BLK] * SCALE2, MASKED))
        top = jnp.max(functools.reduce(jnp.maximum, parts), axis=0, keepdims=True)
        if not first:
            old_top = old[1][block, 0:1]
            top = jnp.maximum(top, old_top)
        weights = [jnp.exp2(piece - top) for piece in parts]
        total = jnp.sum(functools.reduce(jnp.add, weights), axis=0, keepdims=True)
        weights = jnp.concatenate([w.astype(jnp.bfloat16) for w in weights], axis=0)
        acc = jnp.dot(values_t, weights, preferred_element_type=jnp.float32)
        if not first:
            factor = jnp.exp2(old_top - top)
            total = total + old[1][block, 1:2] * factor
            acc = acc + old[0][block] * factor
        if not last:
            refs[0][block] = acc
            refs[1][block, 0:1] = top
            refs[1][block, 1:2] = total
            return carry
        refs[0][block, :HD] = (acc * (1.0 / total)).astype(jnp.bfloat16)
        spread = top + jnp.log2(total)
        high = spread.astype(jnp.bfloat16).astype(jnp.float32)
        rest = spread - high
        middle = rest.astype(jnp.bfloat16).astype(jnp.float32)
        row = lax.broadcasted_iota(jnp.int32, (PIECES, ROWS), 0)
        pieces = jnp.where(row == 0, high, jnp.where(row == 1, middle, jnp.where(row == 2, rest - middle, 0.0)))
        refs[0][block, HD:] = pieces.astype(jnp.bfloat16)
        return carry

    lax.fori_loop(0, LANES, one_block, 0, unroll=UNROLL)


def attend(near, *args):
    out = STATE if near else jax.ShapeDtypeStruct((LANES, HD + PIECES, ROWS), jnp.bfloat16)
    pairs = LANES * ROWS * (5 if near else 4) * BLK
    return pl.pallas_call(
        functools.partial(attend_kernel, near),
        out_shape=out,
        in_specs=[SMEM] + [VREF] * (len(args) - 1),
        out_specs=(VREF, VREF) if near else VREF,
        compiler_params=PARAMS,
        cost_estimate=pl.CostEstimate(flops=4 * pairs * HD, bytes_accessed=3 << 20, transcendentals=pairs),
        name="near" if near else "far",
    )(*args)


def combine_kernel(parts_ref, out_ref):
    spread = []
    for p in range(LANES):
        pieces = parts_ref[p, HD:].astype(jnp.float32)
        spread.append(pieces[0:1] + pieces[1:2] + pieces[2:3])
    top = functools.reduce(jnp.maximum, spread)
    shares = [jnp.exp2(s - top) for s in spread]
    inverse = 1.0 / functools.reduce(jnp.add, shares)
    total = functools.reduce(
        jnp.add, [parts_ref[p, :HD].astype(jnp.float32) * (shares[p] * inverse) for p in range(LANES)]
    )
    for g in range(GROUP):
        head = total[:, g * BLK : (g + 1) * BLK].T.astype(jnp.bfloat16)
        for h in range(HEADS):
            out_ref[h, :, g * HD : (g + 1) * HD] = head


def project_kernel(rows_ref, weight_ref, out_ref):
    depth = rows_ref.shape[2]
    acc = functools.reduce(
        jnp.add,
        [
            jnp.dot(rows_ref[h], weight_ref[h * depth : (h + 1) * depth, :], preferred_element_type=jnp.float32)
            for h in range(HEADS)
        ],
    )
    out_ref[...] = acc.astype(jnp.bfloat16)


def small(kernel, name, shape, dtype, *args, smem=0, params=PARAMS):
    return pl.pallas_call(
        kernel,
        out_shape=jax.ShapeDtypeStruct(shape, dtype),
        in_specs=[SMEM] * smem + [VREF] * (len(args) - smem),
        out_specs=VREF,
        compiler_params=params,
        cost_estimate=pl.CostEstimate(flops=1 << 20, bytes_accessed=1 << 19, transcendentals=0),
        name=name,
    )(*args)


def on_device(queries, keys, values, segments, out_weight):
    plane, lane = lax.axis_index("z"), lax.axis_index(("y", "c"))
    where = jnp.stack([plane, lane]).astype(jnp.int32)
    low = small(low_kernel, "low", (8, BLK), jnp.int32, where, segments.reshape(-1, BLK), smem=1)
    pair_keys, pair_values = lax.all_gather((keys, values), "c", tiled=True)
    own = small(pack_kernel, "pack", (PAIR * BLK, 2 * HD), keys.dtype, pair_keys, pair_values)
    from36 = shift_by_core(own, (3, 6))
    from12 = shift_by_core(own, (1, 2))
    queries, _ = lax.optimization_barrier((queries, own))
    plane_queries = lax.all_gather(queries, ("y", "c"), tiled=True)
    from36, plane_queries, low = lax.optimization_barrier((from36, plane_queries, low))
    one, two = shift_by_core(from36, (1, 1)), shift_by_core(from36, (2, 2))
    common = (where, plane_queries, low)
    state = attend(True, *common, own, from12, from36)
    partial = attend(False, *common, one, two, *state)
    parts = lax.all_to_all(partial, ("y", "c"), 0, 0, tiled=True)
    copies = small(combine_kernel, "combine", (HEADS, BLK, GROUP * HD), jnp.bfloat16, parts)
    attended = lax.all_to_all(copies, "h", 0, 0, tiled=True)
    return small(project_kernel, "project", (BLK, out_weight.shape[1]), jnp.bfloat16, attended, out_weight)


def solution(mesh):
    planes = mesh.shape["seq"] // LANES
    heads = mesh.shape["head"]
    fine = Mesh(mesh.devices.reshape(planes, LANES // PAIR, PAIR, heads), ("z", "y", "c", "h"))
    tokens = ("z", "y", "c")
    return jax.shard_map(
        on_device,
        mesh=fine,
        in_specs=(P(tokens, "h"), P(tokens, "h"), P(tokens, "h"), P(), P(None, "h")),
        out_specs=P(tokens, "h"),
        check_vma=False,
    )
```

```python
import functools

import jax
import jax.numpy as jnp
from jax import lax
from jax.experimental import pallas as pl
from jax.experimental.pallas import tpu as pltpu
from jax.sharding import Mesh, PartitionSpec as P

HD = 128
BLK = 128
GROUP = 4
PAIR = 2
LANES = 4
WINDOW = 31 * BLK
PLANE = LANES * BLK
ROWS = GROUP * BLK
PIECES = 16
HEADS = 8
SEGMENT_VALUES = 6
SCALE2 = float(HD**-0.5 * 1.4426950408889634)
MASKED = -1e30
VMEM = 24 * 1024 * 1024
PARAMS = pltpu.CompilerParams(vmem_limit_bytes=VMEM)
SMEM = pl.BlockSpec(memory_space=pltpu.SMEM)
VREF = pl.BlockSpec(memory_space=pltpu.VMEM)
STATE = (
    jax.ShapeDtypeStruct((LANES, HD, ROWS), jnp.float32),
    jax.ShapeDtypeStruct((LANES, 8, ROWS), jnp.float32),
)


def shift_by_core(block, distances):
    planes, cores = lax.axis_size("z"), lax.axis_size("c")
    route = [
        (z * cores + c, (z + distances[c]) * cores + c) for c in range(cores) for z in range(planes - distances[c])
    ]
    return lax.ppermute(block, ("z", "c"), route)


def low_kernel(where_ref, segment_ref, out_ref):
    segments = segment_ref[...]
    before = [jnp.sum((segments < v).astype(jnp.int32)) for v in range(1, SEGMENT_VALUES)]
    token = lax.broadcasted_iota(jnp.int32, (1, BLK), 1)
    for p in range(LANES):
        own = segment_ref[pl.ds(where_ref[0] * LANES + p, 1), :]
        start = jnp.zeros((1, BLK), jnp.int32)
        for v in range(1, SEGMENT_VALUES):
            start = jnp.where(own == v, before[v - 1], start)
        position = where_ref[0] * PLANE + p * BLK + token
        out_ref[p : p + 1] = jnp.maximum(start, position - (WINDOW - 1))
    out_ref[LANES:] = jnp.zeros((8 - LANES, BLK), jnp.int32)


def attend_kernel(near, where_ref, mine_ref, other_ref, low_ref, *refs):
    first, last = near, not near
    plane, lane = where_ref[0], where_ref[1]
    core = lane % PAIR
    plane_first = plane * PLANE
    side_first = plane_first + (lane - core) * BLK
    if near:
        own_ref, *pairs = refs[:3]
        old, refs = (), refs[3:]
        keys, values, firsts = [own_ref[2 * core]], [own_ref[2 * core + 1]], [side_first + core * BLK]
        distances = (1 + core, 3 + 3 * core)
    else:
        pairs, old, refs = refs[:2], refs[2:4], refs[4:]
        keys, values, firsts = [], [], []
        distances = (4 + 3 * core, 5 + 3 * core)
    for ref, distance in zip(pairs, distances):
        for n in range(PAIR):
            keys.append(ref[2 * n])
            values.append(ref[2 * n + 1])
            firsts.append(side_first + n * BLK - distance * PLANE)
    keys = jnp.concatenate(keys, axis=0)
    values_t = jnp.concatenate(values, axis=0).astype(jnp.float32).T.astype(jnp.bfloat16)
    sub = lax.broadcasted_iota(jnp.int32, (BLK, ROWS), 0)
    token = lax.broadcasted_iota(jnp.int32, (1, ROWS), 1) % BLK
    for index in range(LANES):
        query_ref, of_core = (mine_ref, other_ref)[index // PAIR], index % PAIR
        block = of_core + ((lane - core) if index < PAIR else (PAIR - lane + core))
        rows = slice(of_core * BLK, (of_core + 1) * BLK)
        queries = jnp.concatenate([query_ref[rows, g * HD : (g + 1) * HD] for g in range(GROUP)], axis=0)
        scores = lax.dot_general(keys, queries, (((1,), (1,)), ((), ())), preferred_element_type=jnp.float32)
        low = jnp.concatenate([low_ref[pl.ds(block, 1), :]] * GROUP, axis=1)
        parts = []
        for n, key_first in enumerate(firsts):
            allowed = sub >= low - key_first
            if near and n == 0:
                allowed = allowed & (sub <= plane_first + block * BLK + token - key_first)
            parts.append(jnp.where(allowed, scores[n * BLK : (n + 1) * BLK] * SCALE2, MASKED))
        top = jnp.max(functools.reduce(jnp.maximum, parts), axis=0, keepdims=True)
        if not first:
            old_top = old[1][index, 0:1]
            top = jnp.maximum(top, old_top)
        weights = [jnp.exp2(piece - top) for piece in parts]
        total = jnp.sum(functools.reduce(jnp.add, weights), axis=0, keepdims=True)
        weights = jnp.concatenate([w.astype(jnp.bfloat16) for w in weights], axis=0)
        acc = jnp.dot(values_t, weights, preferred_element_type=jnp.float32)
        if not first:
            factor = jnp.exp2(old_top - top)
            total = total + old[1][index, 1:2] * factor
            acc = acc + old[0][index] * factor
        if not last:
            refs[0][index] = acc
            refs[1][index, 0:1] = top
            refs[1][index, 1:2] = total
            continue
        refs[0][block, :HD] = (acc * (1.0 / total)).astype(jnp.bfloat16)
        spread = top + jnp.log2(total)
        high = spread.astype(jnp.bfloat16).astype(jnp.float32)
        rest = spread - high
        middle = rest.astype(jnp.bfloat16).astype(jnp.float32)
        row = lax.broadcasted_iota(jnp.int32, (PIECES, ROWS), 0)
        pieces = jnp.where(row == 0, high, jnp.where(row == 1, middle, jnp.where(row == 2, rest - middle, 0.0)))
        refs[0][block, HD:] = pieces.astype(jnp.bfloat16)


def attend(near, *args):
    out = STATE if near else jax.ShapeDtypeStruct((LANES, HD + PIECES, ROWS), jnp.bfloat16)
    pairs = LANES * ROWS * (5 if near else 4) * BLK
    return pl.pallas_call(
        functools.partial(attend_kernel, near),
        out_shape=out,
        in_specs=[SMEM] + [VREF] * (len(args) - 1),
        out_specs=(VREF, VREF) if near else VREF,
        compiler_params=PARAMS,
        cost_estimate=pl.CostEstimate(flops=4 * pairs * HD, bytes_accessed=3 << 20, transcendentals=pairs),
        name="near" if near else "far",
    )(*args)


def combine_kernel(parts_ref, out_ref):
    spread = []
    for p in range(LANES):
        pieces = parts_ref[p, HD:].astype(jnp.float32)
        spread.append(pieces[0:1] + pieces[1:2] + pieces[2:3])
    top = functools.reduce(jnp.maximum, spread)
    shares = [jnp.exp2(s - top) for s in spread]
    inverse = 1.0 / functools.reduce(jnp.add, shares)
    total = functools.reduce(
        jnp.add, [parts_ref[p, :HD].astype(jnp.float32) * (shares[p] * inverse) for p in range(LANES)]
    )
    for g in range(GROUP):
        head = total[:, g * BLK : (g + 1) * BLK].T.astype(jnp.bfloat16)
        for h in range(HEADS):
            out_ref[h, :, g * HD : (g + 1) * HD] = head


def project_kernel(rows_ref, weight_ref, out_ref):
    depth = rows_ref.shape[2]
    acc = functools.reduce(
        jnp.add,
        [
            jnp.dot(rows_ref[h], weight_ref[h * depth : (h + 1) * depth, :], preferred_element_type=jnp.float32)
            for h in range(HEADS)
        ],
    )
    out_ref[...] = acc.astype(jnp.bfloat16)


def small(kernel, name, shape, dtype, *args, smem=0, params=PARAMS):
    return pl.pallas_call(
        kernel,
        out_shape=jax.ShapeDtypeStruct(shape, dtype),
        in_specs=[SMEM] * smem + [VREF] * (len(args) - smem),
        out_specs=VREF,
        compiler_params=params,
        cost_estimate=pl.CostEstimate(flops=1 << 20, bytes_accessed=1 << 19, transcendentals=0),
        name=name,
    )(*args)


def on_device(queries, keys, values, segments, out_weight):
    plane, lane = lax.axis_index("z"), lax.axis_index(("y", "c"))
    where = jnp.stack([plane, lane]).astype(jnp.int32)
    low = small(low_kernel, "low", (8, BLK), jnp.int32, where, segments.reshape(-1, BLK), smem=1)
    is_key = lax.broadcasted_iota(jnp.int32, (2, BLK, HD), 0) == 0
    own = lax.all_gather(jnp.where(is_key, keys[None], values[None]), "c", tiled=True)
    from36 = shift_by_core(own, (3, 6))
    from12 = shift_by_core(own, (1, 2))
    queries, _ = lax.optimization_barrier((queries, own))
    mine = lax.all_gather(queries, "c", tiled=True)
    from36, from12, mine, low = lax.optimization_barrier((from36, from12, mine, low))
    other = lax.ppermute(mine, "y", [(0, 1), (1, 0)])
    one, two = shift_by_core(from36, (1, 1)), shift_by_core(from36, (2, 2))
    common = (where, mine, other, low)
    state = attend(True, *common, own, from12, from36)
    partial = attend(False, *common, one, two, *state)
    parts = lax.all_to_all(partial, ("y", "c"), 0, 0, tiled=True)
    copies = small(combine_kernel, "combine", (HEADS, BLK, GROUP * HD), jnp.bfloat16, parts)
    attended = lax.all_to_all(copies, "h", 0, 0, tiled=True)
    return small(project_kernel, "project", (BLK, out_weight.shape[1]), jnp.bfloat16, attended, out_weight)


def solution(mesh):
    planes = mesh.shape["seq"] // LANES
    heads = mesh.shape["head"]
    fine = Mesh(mesh.devices.reshape(planes, LANES // PAIR, PAIR, heads), ("z", "y", "c", "h"))
    tokens = ("z", "y", "c")
    return jax.shard_map(
        on_device,
        mesh=fine,
        in_specs=(P(tokens, "h"), P(tokens, "h"), P(tokens, "h"), P(), P(None, "h")),
        out_specs=P(tokens, "h"),
        check_vma=False,
    )
```

```python
import functools

import jax
import jax.numpy as jnp
from jax import lax
from jax.experimental import pallas as pl
from jax.experimental.pallas import tpu as pltpu
from jax.sharding import Mesh, PartitionSpec as P

HD = 128
BLK = 128
GROUP = 4
PAIR = 2
LANES = 4
WINDOW = 31 * BLK
PLANE = LANES * BLK
ROWS = GROUP * BLK
PIECES = 16
HEADS = 8
SEGMENT_VALUES = 6
SCALE2 = float(HD**-0.5 * 1.4426950408889634)
MASKED = -1e30
VMEM = 24 * 1024 * 1024
PARAMS = pltpu.CompilerParams(vmem_limit_bytes=VMEM)
SMEM = pl.BlockSpec(memory_space=pltpu.SMEM)
VREF = pl.BlockSpec(memory_space=pltpu.VMEM)
STATE = (
    jax.ShapeDtypeStruct((LANES, HD, ROWS), jnp.float32),
    jax.ShapeDtypeStruct((LANES, 8, ROWS), jnp.float32),
)


def shift_by_core(block, distances, crossed=False):
    planes, cores = lax.axis_size("z"), lax.axis_size("c")
    route = [
        (z * cores + c, (z + distances[c]) * cores + (cores - 1 - c if crossed else c))
        for c in range(cores)
        for z in range(planes - distances[c])
    ]
    return lax.ppermute(block, ("z", "c"), route)


def low_kernel(where_ref, segment_ref, out_ref):
    segments = segment_ref[...]
    before = [jnp.sum((segments < v).astype(jnp.int32)) for v in range(1, SEGMENT_VALUES)]
    token = lax.broadcasted_iota(jnp.int32, (1, BLK), 1)
    for p in range(LANES):
        own = segment_ref[pl.ds(where_ref[0] * LANES + p, 1), :]
        start = jnp.zeros((1, BLK), jnp.int32)
        for v in range(1, SEGMENT_VALUES):
            start = jnp.where(own == v, before[v - 1], start)
        position = where_ref[0] * PLANE + p * BLK + token
        out_ref[p : p + 1] = jnp.maximum(start, position - (WINDOW - 1))
    out_ref[LANES:] = jnp.zeros((8 - LANES, BLK), jnp.int32)


def attend_kernel(near, where_ref, mine_ref, other_ref, low_ref, *refs):
    first, last = near, not near
    plane, lane = where_ref[0], where_ref[1]
    core = lane % PAIR
    plane_first = plane * PLANE
    side_first = plane_first + (lane - core) * BLK
    if near:
        own_ref, *pairs = refs[:3]
        old, refs = (), refs[3:]
        keys, values, firsts = [own_ref[2 * core]], [own_ref[2 * core + 1]], [side_first + core * BLK]
        distances = (3 - core, 4 + 2 * core)
    else:
        pairs, old, refs = refs[:2], refs[2:4], refs[4:]
        keys, values, firsts = [], [], []
        distances = (5 + 2 * core, 1 + 7 * core)
    for ref, distance in zip(pairs, distances):
        for n in range(PAIR):
            keys.append(ref[2 * n])
            values.append(ref[2 * n + 1])
            firsts.append(side_first + n * BLK - distance * PLANE)
    keys = jnp.concatenate(keys, axis=0)
    values_t = jnp.concatenate(values, axis=0).astype(jnp.float32).T.astype(jnp.bfloat16)
    sub = lax.broadcasted_iota(jnp.int32, (BLK, ROWS), 0)
    token = lax.broadcasted_iota(jnp.int32, (1, ROWS), 1) % BLK
    for index in range(LANES):
        query_ref, of_core = (mine_ref, other_ref)[index // PAIR], index % PAIR
        block = of_core + ((lane - core) if index < PAIR else (PAIR - lane + core))
        rows = slice(of_core * BLK, (of_core + 1) * BLK)
        queries = jnp.concatenate([query_ref[rows, g * HD : (g + 1) * HD] for g in range(GROUP)], axis=0)
        scores = lax.dot_general(keys, queries, (((1,), (1,)), ((), ())), preferred_element_type=jnp.float32)
        low = jnp.concatenate([low_ref[pl.ds(block, 1), :]] * GROUP, axis=1)
        parts = []
        for n, key_first in enumerate(firsts):
            allowed = sub >= low - key_first
            if near and n == 0:
                allowed = allowed & (sub <= plane_first + block * BLK + token - key_first)
            parts.append(jnp.where(allowed, scores[n * BLK : (n + 1) * BLK] * SCALE2, MASKED))
        top = jnp.max(functools.reduce(jnp.maximum, parts), axis=0, keepdims=True)
        if not first:
            old_top = old[1][index, 0:1]
            top = jnp.maximum(top, old_top)
        weights = [jnp.exp2(piece - top) for piece in parts]
        total = jnp.sum(functools.reduce(jnp.add, weights), axis=0, keepdims=True)
        weights = jnp.concatenate([w.astype(jnp.bfloat16) for w in weights], axis=0)
        acc = jnp.dot(values_t, weights, preferred_element_type=jnp.float32)
        if not first:
            factor = jnp.exp2(old_top - top)
            total = total + old[1][index, 1:2] * factor
            acc = acc + old[0][index] * factor
        if not last:
            refs[0][index] = acc
            refs[1][index, 0:1] = top
            refs[1][index, 1:2] = total
            continue
        refs[0][block, :HD] = (acc * (1.0 / total)).astype(jnp.bfloat16)
        spread = top + jnp.log2(total)
        high = spread.astype(jnp.bfloat16).astype(jnp.float32)
        rest = spread - high
        middle = rest.astype(jnp.bfloat16).astype(jnp.float32)
        row = lax.broadcasted_iota(jnp.int32, (PIECES, ROWS), 0)
        pieces = jnp.where(row == 0, high, jnp.where(row == 1, middle, jnp.where(row == 2, rest - middle, 0.0)))
        refs[0][block, HD:] = pieces.astype(jnp.bfloat16)


def attend(near, *args):
    out = STATE if near else jax.ShapeDtypeStruct((LANES, HD + PIECES, ROWS), jnp.bfloat16)
    pairs = LANES * ROWS * (5 if near else 4) * BLK
    return pl.pallas_call(
        functools.partial(attend_kernel, near),
        out_shape=out,
        in_specs=[SMEM] + [VREF] * (len(args) - 1),
        out_specs=(VREF, VREF) if near else VREF,
        compiler_params=PARAMS,
        cost_estimate=pl.CostEstimate(flops=4 * pairs * HD, bytes_accessed=3 << 20, transcendentals=pairs),
        name="near" if near else "far",
    )(*args)


def combine_kernel(parts_ref, out_ref):
    spread = []
    for p in range(LANES):
        pieces = parts_ref[p, HD:].astype(jnp.float32)
        spread.append(pieces[0:1] + pieces[1:2] + pieces[2:3])
    top = functools.reduce(jnp.maximum, spread)
    shares = [jnp.exp2(s - top) for s in spread]
    inverse = 1.0 / functools.reduce(jnp.add, shares)
    total = functools.reduce(
        jnp.add, [parts_ref[p, :HD].astype(jnp.float32) * (shares[p] * inverse) for p in range(LANES)]
    )
    for g in range(GROUP):
        head = total[:, g * BLK : (g + 1) * BLK].T.astype(jnp.bfloat16)
        for h in range(HEADS):
            out_ref[h, :, g * HD : (g + 1) * HD] = head


def project_kernel(rows_ref, weight_ref, out_ref):
    depth = rows_ref.shape[2]
    acc = functools.reduce(
        jnp.add,
        [
            jnp.dot(rows_ref[h], weight_ref[h * depth : (h + 1) * depth, :], preferred_element_type=jnp.float32)
            for h in range(HEADS)
        ],
    )
    out_ref[...] = acc.astype(jnp.bfloat16)


def small(kernel, name, shape, dtype, *args, smem=0, params=PARAMS):
    return pl.pallas_call(
        kernel,
        out_shape=jax.ShapeDtypeStruct(shape, dtype),
        in_specs=[SMEM] * smem + [VREF] * (len(args) - smem),
        out_specs=VREF,
        compiler_params=params,
        cost_estimate=pl.CostEstimate(flops=1 << 20, bytes_accessed=1 << 19, transcendentals=0),
        name=name,
    )(*args)


def on_device(queries, keys, values, segments, out_weight):
    plane, core, lane = lax.axis_index("z"), lax.axis_index("c"), lax.axis_index(("y", "c"))
    where = jnp.stack([plane, lane]).astype(jnp.int32)
    is_key = lax.broadcasted_iota(jnp.int32, (2, BLK, HD), 0) == 0
    own = lax.all_gather(jnp.where(is_key, keys[None], values[None]), "c", tiled=True)
    come = shift_by_core(own, (3, 2))
    queries, _ = lax.optimization_barrier((queries, own))
    mine = lax.all_gather(queries, "c", tiled=True)
    come, mine, segments = lax.optimization_barrier((come, mine, segments))
    passed = shift_by_core(come, (3, 2), crossed=True)
    low = small(low_kernel, "low", (8, BLK), jnp.int32, where, segments.reshape(-1, BLK), smem=1)
    mine, low = lax.optimization_barrier((mine, low))
    other = lax.ppermute(mine, "y", [(0, 1), (1, 0)])
    passed, low = lax.optimization_barrier((passed, low))
    one = shift_by_core(passed, (1, 1))
    two = shift_by_core(jnp.where(core == 0, own, passed), (1, 2))
    common = (where, mine, other, low)
    state = attend(True, *common, own, come, passed)
    partial = attend(False, *common, one, two, *state)
    parts = lax.all_to_all(partial, ("y", "c"), 0, 0, tiled=True)
    copies = small(combine_kernel, "combine", (HEADS, BLK, GROUP * HD), jnp.bfloat16, parts)
    attended = lax.all_to_all(copies, "h", 0, 0, tiled=True)
    return small(project_kernel, "project", (BLK, out_weight.shape[1]), jnp.bfloat16, attended, out_weight)


def solution(mesh):
    planes = mesh.shape["seq"] // LANES
    heads = mesh.shape["head"]
    fine = Mesh(mesh.devices.reshape(planes, LANES // PAIR, PAIR, heads), ("z", "y", "c", "h"))
    tokens = ("z", "y", "c")
    return jax.shard_map(
        on_device,
        mesh=fine,
        in_specs=(P(tokens, "h"), P(tokens, "h"), P(tokens, "h"), P(), P(None, "h")),
        out_specs=P(tokens, "h"),
        check_vma=False,
    )
```

```python
import functools

import jax
import jax.numpy as jnp
from jax import lax
from jax.experimental import pallas as pl
from jax.experimental.pallas import tpu as pltpu
from jax.sharding import Mesh, PartitionSpec as P

HD = 128
BLK = 128
GROUP = 4
PAIR = 2
LANES = 4
WINDOW = 31 * BLK
PLANE = LANES * BLK
ROWS = GROUP * BLK
PIECES = 16
HEADS = 8
SEGMENT_VALUES = 6
SCALE2 = float(HD**-0.5 * 1.4426950408889634)
MASKED = -1e30
VMEM = 24 * 1024 * 1024
PARAMS = pltpu.CompilerParams(vmem_limit_bytes=VMEM)
SMEM = pl.BlockSpec(memory_space=pltpu.SMEM)
VREF = pl.BlockSpec(memory_space=pltpu.VMEM)
STATE = (
    jax.ShapeDtypeStruct((LANES, HD, ROWS), jnp.float32),
    jax.ShapeDtypeStruct((LANES, 8, ROWS), jnp.float32),
)


def shift_by_core(block, distances):
    planes, cores = lax.axis_size("z"), lax.axis_size("c")
    route = [
        (z * cores + c, (z + distances[c]) * cores + c) for c in range(cores) for z in range(planes - distances[c])
    ]
    return lax.ppermute(block, ("z", "c"), route)


def low_kernel(where_ref, segment_ref, out_ref):
    segments = segment_ref[...]
    before = [jnp.sum((segments < v).astype(jnp.int32)) for v in range(1, SEGMENT_VALUES)]
    token = lax.broadcasted_iota(jnp.int32, (1, BLK), 1)
    for p in range(LANES):
        own = segment_ref[pl.ds(where_ref[0] * LANES + p, 1), :]
        start = jnp.zeros((1, BLK), jnp.int32)
        for v in range(1, SEGMENT_VALUES):
            start = jnp.where(own == v, before[v - 1], start)
        position = where_ref[0] * PLANE + p * BLK + token
        out_ref[p : p + 1] = jnp.maximum(start, position - (WINDOW - 1))
    out_ref[LANES:] = jnp.zeros((8 - LANES, BLK), jnp.int32)


def attend_kernel(near, where_ref, mine_ref, other_ref, low_ref, *refs):
    first, last = near, not near
    plane, lane = where_ref[0], where_ref[1]
    core = lane % PAIR
    plane_first = plane * PLANE
    side_first = plane_first + (lane - core) * BLK
    if near:
        own_ref, *pairs = refs[:3]
        old, refs = (), refs[3:]
        pairs = [(ref, 0) for ref in pairs]
        keys, values, firsts = [own_ref[2 * core]], [own_ref[2 * core + 1]], [side_first + core * BLK]
        distances = (1 + 4 * core, 3 + 4 * core)
    else:
        pairs, old, refs = [(refs[0], 0), (refs[0], 2 * PAIR)], refs[1:3], refs[3:]
        keys, values, firsts = [], [], []
        distances = (2 + 4 * core, 4 + 4 * core)
    for (ref, at), distance in zip(pairs, distances):
        for n in range(PAIR):
            keys.append(ref[at + 2 * n])
            values.append(ref[at + 2 * n + 1])
            firsts.append(side_first + n * BLK - distance * PLANE)
    keys = jnp.concatenate(keys, axis=0)
    values_t = jnp.concatenate(values, axis=0).astype(jnp.float32).T.astype(jnp.bfloat16)
    sub = lax.broadcasted_iota(jnp.int32, (BLK, ROWS), 0)
    token = lax.broadcasted_iota(jnp.int32, (1, ROWS), 1) % BLK
    for index in range(LANES):
        query_ref, of_core = (mine_ref, other_ref)[index // PAIR], index % PAIR
        block = of_core + ((lane - core) if index < PAIR else (PAIR - lane + core))
        rows = slice(of_core * BLK, (of_core + 1) * BLK)
        queries = jnp.concatenate([query_ref[rows, g * HD : (g + 1) * HD] for g in range(GROUP)], axis=0)
        scores = lax.dot_general(keys, queries, (((1,), (1,)), ((), ())), preferred_element_type=jnp.float32)
        low = jnp.concatenate([low_ref[pl.ds(block, 1), :]] * GROUP, axis=1)
        parts = []
        for n, key_first in enumerate(firsts):
            allowed = sub >= low - key_first
            if near and n == 0:
                allowed = allowed & (sub <= plane_first + block * BLK + token - key_first)
            parts.append(jnp.where(allowed, scores[n * BLK : (n + 1) * BLK] * SCALE2, MASKED))
        top = jnp.max(functools.reduce(jnp.maximum, parts), axis=0, keepdims=True)
        if not first:
            old_top = old[1][index, 0:1]
            top = jnp.maximum(top, old_top)
        weights = [jnp.exp2(piece - top) for piece in parts]
        total = jnp.sum(functools.reduce(jnp.add, weights), axis=0, keepdims=True)
        weights = jnp.concatenate([w.astype(jnp.bfloat16) for w in weights], axis=0)
        acc = jnp.dot(values_t, weights, preferred_element_type=jnp.float32)
        if not first:
            factor = jnp.exp2(old_top - top)
            total = total + old[1][index, 1:2] * factor
            acc = acc + old[0][index] * factor
        if not last:
            refs[0][index] = acc
            refs[1][index, 0:1] = top
            refs[1][index, 1:2] = total
            continue
        refs[0][block, :HD] = (acc * (1.0 / total)).astype(jnp.bfloat16)
        spread = top + jnp.log2(total)
        high = spread.astype(jnp.bfloat16).astype(jnp.float32)
        rest = spread - high
        middle = rest.astype(jnp.bfloat16).astype(jnp.float32)
        row = lax.broadcasted_iota(jnp.int32, (PIECES, ROWS), 0)
        pieces = jnp.where(row == 0, high, jnp.where(row == 1, middle, jnp.where(row == 2, rest - middle, 0.0)))
        refs[0][block, HD:] = pieces.astype(jnp.bfloat16)


def attend(near, *args):
    out = STATE if near else jax.ShapeDtypeStruct((LANES, HD + PIECES, ROWS), jnp.bfloat16)
    pairs = LANES * ROWS * (5 if near else 4) * BLK
    return pl.pallas_call(
        functools.partial(attend_kernel, near),
        out_shape=out,
        in_specs=[SMEM] + [VREF] * (len(args) - 1),
        out_specs=(VREF, VREF) if near else VREF,
        compiler_params=PARAMS,
        cost_estimate=pl.CostEstimate(flops=4 * pairs * HD, bytes_accessed=3 << 20, transcendentals=pairs),
        name="near" if near else "far",
    )(*args)


def combine_kernel(parts_ref, out_ref):
    spread = []
    for p in range(LANES):
        pieces = parts_ref[p, HD:].astype(jnp.float32)
        spread.append(pieces[0:1] + pieces[1:2] + pieces[2:3])
    top = functools.reduce(jnp.maximum, spread)
    shares = [jnp.exp2(s - top) for s in spread]
    inverse = 1.0 / functools.reduce(jnp.add, shares)
    total = functools.reduce(
        jnp.add, [parts_ref[p, :HD].astype(jnp.float32) * (shares[p] * inverse) for p in range(LANES)]
    )
    for g in range(GROUP):
        head = total[:, g * BLK : (g + 1) * BLK].T.astype(jnp.bfloat16)
        for h in range(HEADS):
            out_ref[h, :, g * HD : (g + 1) * HD] = head


def project_kernel(rows_ref, weight_ref, out_ref):
    depth = rows_ref.shape[2]
    acc = functools.reduce(
        jnp.add,
        [
            jnp.dot(rows_ref[h], weight_ref[h * depth : (h + 1) * depth, :], preferred_element_type=jnp.float32)
            for h in range(HEADS)
        ],
    )
    out_ref[...] = acc.astype(jnp.bfloat16)


def small(kernel, name, shape, dtype, *args, smem=0, params=PARAMS):
    return pl.pallas_call(
        kernel,
        out_shape=jax.ShapeDtypeStruct(shape, dtype),
        in_specs=[SMEM] * smem + [VREF] * (len(args) - smem),
        out_specs=VREF,
        compiler_params=params,
        cost_estimate=pl.CostEstimate(flops=1 << 20, bytes_accessed=1 << 19, transcendentals=0),
        name=name,
    )(*args)


def on_device(queries, keys, values, segments, out_weight):
    plane, lane = lax.axis_index("z"), lax.axis_index(("y", "c"))
    where = jnp.stack([plane, lane]).astype(jnp.int32)
    is_key = lax.broadcasted_iota(jnp.int32, (2, BLK, HD), 0) == 0
    own = lax.all_gather(jnp.where(is_key, keys[None], values[None]), "c", tiled=True)
    come = shift_by_core(own, (1, 5))
    queries, _ = lax.optimization_barrier((queries, own))
    mine = lax.all_gather(queries, "c", tiled=True)
    come, mine, segments = lax.optimization_barrier((come, mine, segments))
    passed = shift_by_core(come, (2, 2))
    low = small(low_kernel, "low", (8, BLK), jnp.int32, where, segments.reshape(-1, BLK), smem=1)
    mine, low = lax.optimization_barrier((mine, low))
    other = lax.ppermute(mine, "y", [(0, 1), (1, 0)])
    passed, low = lax.optimization_barrier((passed, low))
    last = shift_by_core(jnp.concatenate([come, passed], axis=0), (1, 1))
    common = (where, mine, other, low)
    state = attend(True, *common, own, come, passed)
    partial = attend(False, *common, last, *state)
    parts = lax.all_to_all(partial, ("y", "c"), 0, 0, tiled=True)
    copies = small(combine_kernel, "combine", (HEADS, BLK, GROUP * HD), jnp.bfloat16, parts)
    attended = lax.all_to_all(copies, "h", 0, 0, tiled=True)
    return small(project_kernel, "project", (BLK, out_weight.shape[1]), jnp.bfloat16, attended, out_weight)


def solution(mesh):
    planes = mesh.shape["seq"] // LANES
    heads = mesh.shape["head"]
    fine = Mesh(mesh.devices.reshape(planes, LANES // PAIR, PAIR, heads), ("z", "y", "c", "h"))
    tokens = ("z", "y", "c")
    return jax.shard_map(
        on_device,
        mesh=fine,
        in_specs=(P(tokens, "h"), P(tokens, "h"), P(tokens, "h"), P(), P(None, "h")),
        out_specs=P(tokens, "h"),
        check_vma=False,
    )
```

```python
import functools

import jax
import jax.numpy as jnp
from jax import lax
from jax.experimental import pallas as pl
from jax.experimental.pallas import tpu as pltpu
from jax.sharding import Mesh, PartitionSpec as P

HD = 128
BLK = 128
GROUP = 4
PAIR = 2
LANES = 4
WINDOW = 31 * BLK
PLANE = LANES * BLK
ROWS = GROUP * BLK
PIECES = 16
HEADS = 8
SEGMENT_VALUES = 6
SCALE2 = float(HD**-0.5 * 1.4426950408889634)
MASKED = -1e30
AHEAD = 2
VMEM = 24 * 1024 * 1024
PARAMS = pltpu.CompilerParams(vmem_limit_bytes=VMEM)
SMEM = pl.BlockSpec(memory_space=pltpu.SMEM)
VREF = pl.BlockSpec(memory_space=pltpu.VMEM)
STATE = (
    jax.ShapeDtypeStruct((LANES, HD, ROWS), jnp.float32),
    jax.ShapeDtypeStruct((LANES, 8, ROWS), jnp.float32),
)


def shift_by_core(block, distances):
    planes, cores = lax.axis_size("z"), lax.axis_size("c")
    route = [
        (z * cores + c, (z + distances[c]) * cores + c) for c in range(cores) for z in range(planes - distances[c])
    ]
    return lax.ppermute(block, ("z", "c"), route)


def low_kernel(where_ref, segment_ref, out_ref):
    segments = segment_ref[...]
    before = [jnp.sum((segments < v).astype(jnp.int32)) for v in range(1, SEGMENT_VALUES)]
    token = lax.broadcasted_iota(jnp.int32, (1, BLK), 1)
    for p in range(LANES):
        own = segment_ref[pl.ds(where_ref[0] * LANES + p, 1), :]
        start = jnp.zeros((1, BLK), jnp.int32)
        for v in range(1, SEGMENT_VALUES):
            start = jnp.where(own == v, before[v - 1], start)
        position = where_ref[0] * PLANE + p * BLK + token
        out_ref[p : p + 1] = jnp.maximum(start, position - (WINDOW - 1))
    out_ref[LANES:] = jnp.zeros((8 - LANES, BLK), jnp.int32)


def attend_kernel(near, where_ref, mine_ref, other_ref, low_ref, *refs):
    first, last = near, not near
    plane, lane = where_ref[0], where_ref[1]
    core = lane % PAIR
    plane_first = plane * PLANE
    side_first = plane_first + (lane - core) * BLK
    if near:
        own_ref, *pairs = refs[:3]
        old, refs = (), refs[3:]
        pairs = [(ref, 0) for ref in pairs]
        keys, values, firsts = [own_ref[2 * core]], [own_ref[2 * core + 1]], [side_first + core * BLK]
        distances = (1 + 4 * core, 3 + 4 * core)
    else:
        pairs, old, refs = [(refs[0], 0), (refs[0], 2 * PAIR)], refs[1:3], refs[3:]
        keys, values, firsts = [], [], []
        distances = (2 + 4 * core, 4 + 4 * core)
    for (ref, at), distance in zip(pairs, distances):
        for n in range(PAIR):
            keys.append(ref[at + 2 * n])
            values.append(ref[at + 2 * n + 1])
            firsts.append(side_first + n * BLK - distance * PLANE)
    keys = jnp.concatenate(keys, axis=0)
    values_t = jnp.concatenate(values, axis=0).astype(jnp.float32).T.astype(jnp.bfloat16)
    sub = lax.broadcasted_iota(jnp.int32, (BLK, BLK), 0)
    token = lax.broadcasted_iota(jnp.int32, (1, BLK), 1)

    def scores_of(index):
        query_ref, of_core = (mine_ref, other_ref)[index // PAIR], index % PAIR
        rows = slice(of_core * BLK, (of_core + 1) * BLK)
        queries = jnp.concatenate([query_ref[rows, g * HD : (g + 1) * HD] for g in range(GROUP)], axis=0)
        return lax.dot_general(keys, queries, (((1,), (1,)), ((), ())), preferred_element_type=jnp.float32)

    ahead = [scores_of(index) for index in range(AHEAD)]
    for index in range(LANES):
        if index + AHEAD < LANES:
            ahead.append(scores_of(index + AHEAD))
        scores = ahead[index]
        block = index % PAIR + ((lane - core) if index < PAIR else (PAIR - lane + core))
        low = low_ref[pl.ds(block, 1), :]
        parts = []
        for n, key_first in enumerate(firsts):
            allowed = sub >= low - key_first
            if near and n == 0:
                allowed = allowed & (sub <= plane_first + block * BLK + token - key_first)
            bias = jnp.where(allowed, 0.0, MASKED)
            bias = jnp.concatenate([bias] * GROUP, axis=1)
            parts.append(scores[n * BLK : (n + 1) * BLK] * SCALE2 + bias)
        top = jnp.max(functools.reduce(jnp.maximum, parts), axis=0, keepdims=True)
        if not first:
            old_top = old[1][index, 0:1]
            top = jnp.maximum(top, old_top)
        weights = [jnp.exp2(piece - top) for piece in parts]
        total = jnp.sum(functools.reduce(jnp.add, weights), axis=0, keepdims=True)
        weights = jnp.concatenate([w.astype(jnp.bfloat16) for w in weights], axis=0)
        acc = jnp.dot(values_t, weights, preferred_element_type=jnp.float32)
        if not first:
            factor = jnp.exp2(old_top - top)
            total = total + old[1][index, 1:2] * factor
            acc = acc + old[0][index] * factor
        if not last:
            refs[0][index] = acc
            refs[1][index, 0:1] = top
            refs[1][index, 1:2] = total
            continue
        refs[0][block, :HD] = (acc * (1.0 / total)).astype(jnp.bfloat16)
        spread = top + jnp.log2(total)
        high = spread.astype(jnp.bfloat16).astype(jnp.float32)
        rest = spread - high
        middle = rest.astype(jnp.bfloat16).astype(jnp.float32)
        row = lax.broadcasted_iota(jnp.int32, (PIECES, ROWS), 0)
        pieces = jnp.where(row == 0, high, jnp.where(row == 1, middle, jnp.where(row == 2, rest - middle, 0.0)))
        refs[0][block, HD:] = pieces.astype(jnp.bfloat16)


def attend(near, *args):
    out = STATE if near else jax.ShapeDtypeStruct((LANES, HD + PIECES, ROWS), jnp.bfloat16)
    pairs = LANES * ROWS * (5 if near else 4) * BLK
    return pl.pallas_call(
        functools.partial(attend_kernel, near),
        out_shape=out,
        in_specs=[SMEM] + [VREF] * (len(args) - 1),
        out_specs=(VREF, VREF) if near else VREF,
        compiler_params=PARAMS,
        cost_estimate=pl.CostEstimate(flops=4 * pairs * HD, bytes_accessed=3 << 20, transcendentals=pairs),
        name="near" if near else "far",
    )(*args)


def combine_kernel(parts_ref, out_ref):
    spread = []
    for p in range(LANES):
        pieces = parts_ref[p, HD:].astype(jnp.float32)
        spread.append(pieces[0:1] + pieces[1:2] + pieces[2:3])
    top = functools.reduce(jnp.maximum, spread)
    shares = [jnp.exp2(s - top) for s in spread]
    inverse = 1.0 / functools.reduce(jnp.add, shares)
    total = functools.reduce(
        jnp.add, [parts_ref[p, :HD].astype(jnp.float32) * (shares[p] * inverse) for p in range(LANES)]
    )
    for g in range(GROUP):
        head = total[:, g * BLK : (g + 1) * BLK].T.astype(jnp.bfloat16)
        for h in range(HEADS):
            out_ref[h, :, g * HD : (g + 1) * HD] = head


def project_kernel(rows_ref, weight_ref, out_ref):
    depth = rows_ref.shape[2]
    acc = functools.reduce(
        jnp.add,
        [
            jnp.dot(rows_ref[h], weight_ref[h * depth : (h + 1) * depth, :], preferred_element_type=jnp.float32)
            for h in range(HEADS)
        ],
    )
    out_ref[...] = acc.astype(jnp.bfloat16)


def small(kernel, name, shape, dtype, *args, smem=0, params=PARAMS):
    return pl.pallas_call(
        kernel,
        out_shape=jax.ShapeDtypeStruct(shape, dtype),
        in_specs=[SMEM] * smem + [VREF] * (len(args) - smem),
        out_specs=VREF,
        compiler_params=params,
        cost_estimate=pl.CostEstimate(flops=1 << 20, bytes_accessed=1 << 19, transcendentals=0),
        name=name,
    )(*args)


def on_device(queries, keys, values, segments, out_weight):
    plane, lane = lax.axis_index("z"), lax.axis_index(("y", "c"))
    where = jnp.stack([plane, lane]).astype(jnp.int32)
    is_key = lax.broadcasted_iota(jnp.int32, (2, BLK, HD), 0) == 0
    own = lax.all_gather(jnp.where(is_key, keys[None], values[None]), "c", tiled=True)
    come = shift_by_core(own, (1, 5))
    queries, _ = lax.optimization_barrier((queries, own))
    mine = lax.all_gather(queries, "c", tiled=True)
    come, mine, segments = lax.optimization_barrier((come, mine, segments))
    passed = shift_by_core(come, (2, 2))
    low = small(low_kernel, "low", (8, BLK), jnp.int32, where, segments.reshape(-1, BLK), smem=1)
    mine, low = lax.optimization_barrier((mine, low))
    other = lax.ppermute(mine, "y", [(0, 1), (1, 0)])
    passed, low = lax.optimization_barrier((passed, low))
    last = shift_by_core(jnp.concatenate([come, passed], axis=0), (1, 1))
    common = (where, mine, other, low)
    state = attend(True, *common, own, come, passed)
    partial = attend(False, *common, last, *state)
    parts = lax.all_to_all(partial, ("y", "c"), 0, 0, tiled=True)
    copies = small(combine_kernel, "combine", (HEADS, BLK, GROUP * HD), jnp.bfloat16, parts)
    attended = lax.all_to_all(copies, "h", 0, 0, tiled=True)
    return small(project_kernel, "project", (BLK, out_weight.shape[1]), jnp.bfloat16, attended, out_weight)


def solution(mesh):
    planes = mesh.shape["seq"] // LANES
    heads = mesh.shape["head"]
    fine = Mesh(mesh.devices.reshape(planes, LANES // PAIR, PAIR, heads), ("z", "y", "c", "h"))
    tokens = ("z", "y", "c")
    return jax.shard_map(
        on_device,
        mesh=fine,
        in_specs=(P(tokens, "h"), P(tokens, "h"), P(tokens, "h"), P(), P(None, "h")),
        out_specs=P(tokens, "h"),
        check_vma=False,
    )
```

```python
import functools

import jax
import jax.numpy as jnp
from jax import lax
from jax.experimental import pallas as pl
from jax.experimental.pallas import tpu as pltpu
from jax.sharding import Mesh, PartitionSpec as P

HD = 128
BLK = 128
GROUP = 4
PAIR = 2
LANES = 4
WINDOW = 31 * BLK
PLANE = LANES * BLK
ROWS = GROUP * BLK
PIECES = 16
HEADS = 8
SEGMENT_VALUES = 6
SCALE2 = float(HD**-0.5 * 1.4426950408889634)
MASKED = -1e30
AHEAD = 2
VMEM = 24 * 1024 * 1024
PARAMS = pltpu.CompilerParams(vmem_limit_bytes=VMEM)
SMEM = pl.BlockSpec(memory_space=pltpu.SMEM)
VREF = pl.BlockSpec(memory_space=pltpu.VMEM)
STATE = (
    jax.ShapeDtypeStruct((LANES, HD, ROWS), jnp.float32),
    jax.ShapeDtypeStruct((LANES, 8, ROWS), jnp.float32),
)


def shift_by_core(block, distances):
    planes, cores = lax.axis_size("z"), lax.axis_size("c")
    route = [
        (z * cores + c, (z + distances[c]) * cores + c) for c in range(cores) for z in range(planes - distances[c])
    ]
    return lax.ppermute(block, ("z", "c"), route)


def place_kernel(place_ref, out_ref):
    for i in range(2):
        out_ref[i] = place_ref[i]


def low_kernel(where_ref, segment_ref, out_ref):
    segments = segment_ref[...]
    before = [jnp.sum((segments < v).astype(jnp.int32)) for v in range(1, SEGMENT_VALUES)]
    token = lax.broadcasted_iota(jnp.int32, (1, BLK), 1)
    for p in range(LANES):
        own = segment_ref[pl.ds(where_ref[0] * LANES + p, 1), :]
        start = jnp.zeros((1, BLK), jnp.int32)
        for v in range(1, SEGMENT_VALUES):
            start = jnp.where(own == v, before[v - 1], start)
        position = where_ref[0] * PLANE + p * BLK + token
        out_ref[p : p + 1] = jnp.maximum(start, position - (WINDOW - 1))
    out_ref[LANES:] = jnp.zeros((8 - LANES, BLK), jnp.int32)


def attend_kernel(near, where_ref, mine_ref, other_ref, low_ref, *refs):
    first, last = near, not near
    plane, lane = where_ref[0], where_ref[1]
    core = lane % PAIR
    plane_first = plane * PLANE
    side_first = plane_first + (lane - core) * BLK
    if near:
        own_ref, *pairs = refs[:3]
        old, refs = (), refs[3:]
        pairs = [(ref, 0) for ref in pairs]
        keys, values, firsts = [own_ref[2 * core]], [own_ref[2 * core + 1]], [side_first + core * BLK]
        distances = (1 + 4 * core, 3 + 4 * core)
    else:
        pairs, old, refs = [(refs[0], 0), (refs[0], 2 * PAIR)], refs[1:3], refs[3:]
        keys, values, firsts = [], [], []
        distances = (2 + 4 * core, 4 + 4 * core)
    for (ref, at), distance in zip(pairs, distances):
        for n in range(PAIR):
            keys.append(ref[at + 2 * n])
            values.append(ref[at + 2 * n + 1])
            firsts.append(side_first + n * BLK - distance * PLANE)
    keys = jnp.concatenate(keys, axis=0)
    values_t = jnp.concatenate(values, axis=0).astype(jnp.float32).T.astype(jnp.bfloat16)
    sub = lax.broadcasted_iota(jnp.int32, (BLK, BLK), 0)
    token = lax.broadcasted_iota(jnp.int32, (1, BLK), 1)

    def scores_of(index):
        query_ref, of_core = (mine_ref, other_ref)[index // PAIR], index % PAIR
        rows = slice(of_core * BLK, (of_core + 1) * BLK)
        queries = jnp.concatenate([query_ref[rows, g * HD : (g + 1) * HD] for g in range(GROUP)], axis=0)
        return lax.dot_general(keys, queries, (((1,), (1,)), ((), ())), preferred_element_type=jnp.float32)

    ahead = [scores_of(index) for index in range(AHEAD)]
    for index in range(LANES):
        if index + AHEAD < LANES:
            ahead.append(scores_of(index + AHEAD))
        scores = ahead[index]
        block = index % PAIR + ((lane - core) if index < PAIR else (PAIR - lane + core))
        low = low_ref[pl.ds(block, 1), :]
        parts = []
        for n, key_first in enumerate(firsts):
            allowed = sub >= low - key_first
            if near and n == 0:
                allowed = allowed & (sub <= plane_first + block * BLK + token - key_first)
            bias = jnp.where(allowed, 0.0, MASKED)
            bias = jnp.concatenate([bias] * GROUP, axis=1)
            parts.append(scores[n * BLK : (n + 1) * BLK] * SCALE2 + bias)
        top = jnp.max(functools.reduce(jnp.maximum, parts), axis=0, keepdims=True)
        if not first:
            old_top = old[1][index, 0:1]
            top = jnp.maximum(top, old_top)
        weights = [jnp.exp2(piece - top) for piece in parts]
        total = jnp.sum(functools.reduce(jnp.add, weights), axis=0, keepdims=True)
        weights = jnp.concatenate([w.astype(jnp.bfloat16) for w in weights], axis=0)
        acc = jnp.dot(values_t, weights, preferred_element_type=jnp.float32)
        if not first:
            factor = jnp.exp2(old_top - top)
            total = total + old[1][index, 1:2] * factor
            acc = acc + old[0][index] * factor
        if not last:
            refs[0][index] = acc
            refs[1][index, 0:1] = top
            refs[1][index, 1:2] = total
            continue
        refs[0][block, :HD] = (acc * (1.0 / total)).astype(jnp.bfloat16)
        spread = top + jnp.log2(total)
        high = spread.astype(jnp.bfloat16).astype(jnp.float32)
        rest = spread - high
        middle = rest.astype(jnp.bfloat16).astype(jnp.float32)
        row = lax.broadcasted_iota(jnp.int32, (PIECES, ROWS), 0)
        pieces = jnp.where(row == 0, high, jnp.where(row == 1, middle, jnp.where(row == 2, rest - middle, 0.0)))
        refs[0][block, HD:] = pieces.astype(jnp.bfloat16)


def attend(near, *args):
    out = STATE if near else jax.ShapeDtypeStruct((LANES, HD + PIECES, ROWS), jnp.bfloat16)
    pairs = LANES * ROWS * (5 if near else 4) * BLK
    return pl.pallas_call(
        functools.partial(attend_kernel, near),
        out_shape=out,
        in_specs=[SMEM] + [VREF] * (len(args) - 1),
        out_specs=(VREF, VREF) if near else VREF,
        compiler_params=PARAMS,
        cost_estimate=pl.CostEstimate(flops=4 * pairs * HD, bytes_accessed=3 << 20, transcendentals=pairs),
        name="near" if near else "far",
    )(*args)


def combine_kernel(parts_ref, out_ref):
    spread = []
    for p in range(LANES):
        pieces = parts_ref[p, HD:].astype(jnp.float32)
        spread.append(pieces[0:1] + pieces[1:2] + pieces[2:3])
    top = functools.reduce(jnp.maximum, spread)
    shares = [jnp.exp2(s - top) for s in spread]
    inverse = 1.0 / functools.reduce(jnp.add, shares)
    total = functools.reduce(
        jnp.add, [parts_ref[p, :HD].astype(jnp.float32) * (shares[p] * inverse) for p in range(LANES)]
    )
    for g in range(GROUP):
        head = total[:, g * BLK : (g + 1) * BLK].T.astype(jnp.bfloat16)
        for h in range(HEADS):
            out_ref[h, :, g * HD : (g + 1) * HD] = head


def project_kernel(rows_ref, weight_ref, out_ref):
    depth = rows_ref.shape[2]
    acc = functools.reduce(
        jnp.add,
        [
            jnp.dot(rows_ref[h], weight_ref[h * depth : (h + 1) * depth, :], preferred_element_type=jnp.float32)
            for h in range(HEADS)
        ],
    )
    out_ref[...] = acc.astype(jnp.bfloat16)


def small(kernel, name, shape, dtype, *args, smem=0, out=VREF):
    return pl.pallas_call(
        kernel,
        out_shape=jax.ShapeDtypeStruct(shape, dtype),
        in_specs=[SMEM] * smem + [VREF] * (len(args) - smem),
        out_specs=out,
        compiler_params=PARAMS,
        cost_estimate=pl.CostEstimate(flops=1 << 20, bytes_accessed=1 << 19, transcendentals=0),
        name=name,
    )(*args)


def on_device(queries, keys, values, segments, out_weight):
    is_key = lax.broadcasted_iota(jnp.int32, (2, BLK, HD), 0) == 0
    own = lax.all_gather(jnp.where(is_key, keys[None], values[None]), "c", tiled=True)
    come = shift_by_core(own, (1, 5))
    queries, _ = lax.optimization_barrier((queries, own))
    mine = lax.all_gather(queries, "c", tiled=True)
    place = jnp.stack([lax.axis_index("z"), lax.axis_index(("y", "c"))]).astype(jnp.int32)
    come, mine, place = lax.optimization_barrier((come, mine, place))
    passed = shift_by_core(come, (2, 2))
    where = small(place_kernel, "place", (2,), jnp.int32, place, smem=1, out=SMEM)
    mine, where = lax.optimization_barrier((mine, where))
    other = lax.ppermute(mine, "y", [(0, 1), (1, 0)])
    passed, segments, where = lax.optimization_barrier((passed, segments, where))
    last = shift_by_core(jnp.concatenate([come, passed], axis=0), (1, 1))
    low = small(low_kernel, "low", (8, BLK), jnp.int32, where, segments.reshape(-1, BLK), smem=1)
    common = (where, mine, other, low)
    state = attend(True, *common, own, come, passed)
    partial = attend(False, *common, last, *state)
    parts = lax.all_to_all(partial, ("y", "c"), 0, 0, tiled=True)
    copies = small(combine_kernel, "combine", (HEADS, BLK, GROUP * HD), jnp.bfloat16, parts)
    attended = lax.all_to_all(copies, "h", 0, 0, tiled=True)
    return small(project_kernel, "project", (BLK, out_weight.shape[1]), jnp.bfloat16, attended, out_weight)


def solution(mesh):
    planes = mesh.shape["seq"] // LANES
    heads = mesh.shape["head"]
    fine = Mesh(mesh.devices.reshape(planes, LANES // PAIR, PAIR, heads), ("z", "y", "c", "h"))
    tokens = ("z", "y", "c")
    return jax.shard_map(
        on_device,
        mesh=fine,
        in_specs=(P(tokens, "h"), P(tokens, "h"), P(tokens, "h"), P(), P(None, "h")),
        out_specs=P(tokens, "h"),
        check_vma=False,
    )
```

```python
import functools

import jax
import jax.numpy as jnp
from jax import lax
from jax.experimental import pallas as pl
from jax.experimental.pallas import tpu as pltpu
from jax.sharding import Mesh, PartitionSpec as P

HD = 128
BLK = 128
GROUP = 4
PAIR = 2
LANES = 4
WINDOW = 31 * BLK
PLANE = LANES * BLK
ROWS = GROUP * BLK
PIECES = 16
HEADS = 8
SEGMENT_VALUES = 6
SCALE2 = float(HD**-0.5 * 1.4426950408889634)
MASKED = -1e30
AHEAD = 2
VMEM = 24 * 1024 * 1024
PARAMS = pltpu.CompilerParams(vmem_limit_bytes=VMEM)
SMEM = pl.BlockSpec(memory_space=pltpu.SMEM)
VREF = pl.BlockSpec(memory_space=pltpu.VMEM)
STATE = (
    jax.ShapeDtypeStruct((LANES, HD, ROWS), jnp.float32),
    jax.ShapeDtypeStruct((LANES, 8, ROWS), jnp.float32),
)


def shift_by_core(block, distances):
    planes, cores = lax.axis_size("z"), lax.axis_size("c")
    route = [
        (z * cores + c, (z + distances[c]) * cores + c) for c in range(cores) for z in range(planes - distances[c])
    ]
    return lax.ppermute(block, ("z", "c"), route)


def floor_kernel(where_ref, out_ref):
    row = lax.broadcasted_iota(jnp.int32, (8, BLK), 0)
    token = lax.broadcasted_iota(jnp.int32, (8, BLK), 1)
    out_ref[...] = where_ref[0] * PLANE + row * BLK + token - (WINDOW - 1)


def low_kernel(where_ref, segment_ref, floor_ref, out_ref):
    segments = segment_ref[...]
    before = [jnp.sum((segments < v).astype(jnp.int32)) for v in range(1, SEGMENT_VALUES)]
    for p in range(LANES):
        own = segment_ref[pl.ds(where_ref[0] * LANES + p, 1), :]
        start = jnp.zeros((1, BLK), jnp.int32)
        for v in range(1, SEGMENT_VALUES):
            start = jnp.where(own == v, before[v - 1], start)
        out_ref[p : p + 1] = jnp.maximum(start, floor_ref[p : p + 1])
    out_ref[LANES:] = floor_ref[LANES:]


def attend_kernel(near, where_ref, mine_ref, other_ref, low_ref, *refs):
    first, last = near, not near
    plane, lane = where_ref[0], where_ref[1]
    core = lane % PAIR
    plane_first = plane * PLANE
    side_first = plane_first + (lane - core) * BLK
    if near:
        own_ref, *pairs = refs[:3]
        old, refs = (), refs[3:]
        pairs = [(ref, 0) for ref in pairs]
        keys, values, firsts = [own_ref[2 * core]], [own_ref[2 * core + 1]], [side_first + core * BLK]
        distances = (1 + 4 * core, 3 + 4 * core)
    else:
        pairs, old, refs = [(refs[0], 0), (refs[0], 2 * PAIR)], refs[1:3], refs[3:]
        keys, values, firsts = [], [], []
        distances = (2 + 4 * core, 4 + 4 * core)
    for (ref, at), distance in zip(pairs, distances):
        for n in range(PAIR):
            keys.append(ref[at + 2 * n])
            values.append(ref[at + 2 * n + 1])
            firsts.append(side_first + n * BLK - distance * PLANE)
    keys = jnp.concatenate(keys, axis=0)
    values_t = jnp.concatenate(values, axis=0).astype(jnp.float32).T.astype(jnp.bfloat16)
    sub = lax.broadcasted_iota(jnp.int32, (BLK, BLK), 0)
    token = lax.broadcasted_iota(jnp.int32, (1, BLK), 1)

    def scores_of(index):
        query_ref, of_core = (mine_ref, other_ref)[index // PAIR], index % PAIR
        rows = slice(of_core * BLK, (of_core + 1) * BLK)
        queries = jnp.concatenate([query_ref[rows, g * HD : (g + 1) * HD] for g in range(GROUP)], axis=0)
        return lax.dot_general(keys, queries, (((1,), (1,)), ((), ())), preferred_element_type=jnp.float32)

    ahead = [scores_of(index) for index in range(AHEAD)]
    for index in range(LANES):
        if index + AHEAD < LANES:
            ahead.append(scores_of(index + AHEAD))
        scores = ahead[index]
        block = index % PAIR + ((lane - core) if index < PAIR else (PAIR - lane + core))
        low = low_ref[pl.ds(block, 1), :]
        parts = []
        for n, key_first in enumerate(firsts):
            allowed = sub >= low - key_first
            if near and n == 0:
                allowed = allowed & (sub <= plane_first + block * BLK + token - key_first)
            bias = jnp.where(allowed, 0.0, MASKED)
            bias = jnp.concatenate([bias] * GROUP, axis=1)
            parts.append(scores[n * BLK : (n + 1) * BLK] * SCALE2 + bias)
        top = jnp.max(functools.reduce(jnp.maximum, parts), axis=0, keepdims=True)
        if not first:
            old_top = old[1][index, 0:1]
            top = jnp.maximum(top, old_top)
        weights = [jnp.exp2(piece - top) for piece in parts]
        total = jnp.sum(functools.reduce(jnp.add, weights), axis=0, keepdims=True)
        weights = jnp.concatenate([w.astype(jnp.bfloat16) for w in weights], axis=0)
        acc = jnp.dot(values_t, weights, preferred_element_type=jnp.float32)
        if not first:
            factor = jnp.exp2(old_top - top)
            total = total + old[1][index, 1:2] * factor
            acc = acc + old[0][index] * factor
        if not last:
            refs[0][index] = acc
            refs[1][index, 0:1] = top
            refs[1][index, 1:2] = total
            continue
        refs[0][block, :HD] = (acc * (1.0 / total)).astype(jnp.bfloat16)
        spread = top + jnp.log2(total)
        high = spread.astype(jnp.bfloat16).astype(jnp.float32)
        rest = spread - high
        middle = rest.astype(jnp.bfloat16).astype(jnp.float32)
        row = lax.broadcasted_iota(jnp.int32, (PIECES, ROWS), 0)
        pieces = jnp.where(row == 0, high, jnp.where(row == 1, middle, jnp.where(row == 2, rest - middle, 0.0)))
        refs[0][block, HD:] = pieces.astype(jnp.bfloat16)


def attend(near, *args):
    out = STATE if near else jax.ShapeDtypeStruct((LANES, HD + PIECES, ROWS), jnp.bfloat16)
    pairs = LANES * ROWS * (5 if near else 4) * BLK
    return pl.pallas_call(
        functools.partial(attend_kernel, near),
        out_shape=out,
        in_specs=[SMEM] + [VREF] * (len(args) - 1),
        out_specs=(VREF, VREF) if near else VREF,
        compiler_params=PARAMS,
        cost_estimate=pl.CostEstimate(flops=4 * pairs * HD, bytes_accessed=3 << 20, transcendentals=pairs),
        name="near" if near else "far",
    )(*args)


def combine_kernel(parts_ref, out_ref):
    spread = []
    for p in range(LANES):
        pieces = parts_ref[p, HD:].astype(jnp.float32)
        spread.append(pieces[0:1] + pieces[1:2] + pieces[2:3])
    top = functools.reduce(jnp.maximum, spread)
    shares = [jnp.exp2(s - top) for s in spread]
    inverse = 1.0 / functools.reduce(jnp.add, shares)
    total = functools.reduce(
        jnp.add, [parts_ref[p, :HD].astype(jnp.float32) * (shares[p] * inverse) for p in range(LANES)]
    )
    for g in range(GROUP):
        head = total[:, g * BLK : (g + 1) * BLK].T.astype(jnp.bfloat16)
        for h in range(HEADS):
            out_ref[h, :, g * HD : (g + 1) * HD] = head


def project_kernel(rows_ref, weight_ref, out_ref):
    depth = rows_ref.shape[2]
    acc = functools.reduce(
        jnp.add,
        [
            jnp.dot(rows_ref[h], weight_ref[h * depth : (h + 1) * depth, :], preferred_element_type=jnp.float32)
            for h in range(HEADS)
        ],
    )
    out_ref[...] = acc.astype(jnp.bfloat16)


def small(kernel, name, shape, dtype, *args, smem=0):
    return pl.pallas_call(
        kernel,
        out_shape=jax.ShapeDtypeStruct(shape, dtype),
        in_specs=[SMEM] * smem + [VREF] * (len(args) - smem),
        out_specs=VREF,
        compiler_params=PARAMS,
        cost_estimate=pl.CostEstimate(flops=1 << 20, bytes_accessed=1 << 19, transcendentals=0),
        name=name,
    )(*args)


def on_device(queries, keys, values, segments, out_weight):
    is_key = lax.broadcasted_iota(jnp.int32, (2, BLK, HD), 0) == 0
    own = lax.all_gather(jnp.where(is_key, keys[None], values[None]), "c", tiled=True)
    come = shift_by_core(own, (1, 5))
    queries, _ = lax.optimization_barrier((queries, own))
    mine = lax.all_gather(queries, "c", tiled=True)
    where = jnp.stack([lax.axis_index("z"), lax.axis_index(("y", "c"))]).astype(jnp.int32)
    come, mine, where = lax.optimization_barrier((come, mine, where))
    passed = shift_by_core(come, (2, 2))
    floor = small(floor_kernel, "floor", (8, BLK), jnp.int32, where, smem=1)
    mine, floor = lax.optimization_barrier((mine, floor))
    other = lax.ppermute(mine, "y", [(0, 1), (1, 0)])
    passed, segments, floor = lax.optimization_barrier((passed, segments, floor))
    last = shift_by_core(jnp.concatenate([come, passed], axis=0), (1, 1))
    low = small(low_kernel, "low", (8, BLK), jnp.int32, where, segments.reshape(-1, BLK), floor, smem=1)
    common = (where, mine, other, low)
    state = attend(True, *common, own, come, passed)
    partial = attend(False, *common, last, *state)
    parts = lax.all_to_all(partial, ("y", "c"), 0, 0, tiled=True)
    copies = small(combine_kernel, "combine", (HEADS, BLK, GROUP * HD), jnp.bfloat16, parts)
    attended = lax.all_to_all(copies, "h", 0, 0, tiled=True)
    return small(project_kernel, "project", (BLK, out_weight.shape[1]), jnp.bfloat16, attended, out_weight)


def solution(mesh):
    planes = mesh.shape["seq"] // LANES
    heads = mesh.shape["head"]
    fine = Mesh(mesh.devices.reshape(planes, LANES // PAIR, PAIR, heads), ("z", "y", "c", "h"))
    tokens = ("z", "y", "c")
    return jax.shard_map(
        on_device,
        mesh=fine,
        in_specs=(P(tokens, "h"), P(tokens, "h"), P(tokens, "h"), P(), P(None, "h")),
        out_specs=P(tokens, "h"),
        check_vma=False,
    )
```
